32 devices in a mesh: rep: 2 (over x), grp: 8 (over z, y), tp: 2 (over core).
Axes of the slice: x: 2, y: 2, z: 4, core: 2. Of those that a mesh axis runs over, the one named last changes fastest.
Arguments:
- hidden: bfloat16 [4, 3584, 8192], P(None, ('rep', 'grp'), 'tp'), parts along dimension 1, may hold values from -6 to 6
- base_weight: bfloat16 [8192, 512], P('tp'), may hold values from -0.0625 to 0.0625
- pool_down: bfloat16 [8, 8192, 64], P('grp', 'tp'), may hold values from -0.0625 to 0.0625
- pool_up: bfloat16 [8, 64, 512], P('grp'), may hold values from -0.75 to 0.75
- adapter_home: int32 [8], replicated, may hold values from 0 to 7, each once
- block_adapter: int32 [16, 2], P('rep'), parts along dimension 0, may hold values from 0 to 7
- block_count: int32 [16], P('rep'), parts along dimension 0, may hold values from 1 to 2, as said below
Outputs:
- projected: bfloat16 [4, 3584, 512], P(None, ('rep', 'grp'), 'tp'), parts along dimension 1
The draws below stay inside these ranges and needn't reach their ends.
There are 2 independent parts, one for each index of `rep`. The reference program is written for one: setup_inputs(seed, part) draws one part's arguments, and reference() takes and returns one part's arrays. A program takes and returns all parts, laid end to end along the dimension named above; an argument that names none is the same for every part. Nothing has to cross between parts.
Inputs may be any that keep to these rules, and one draw needn't show every extreme that they name: `block_count`: every group uses 1 to 2 blocks and some group uses all 2; entries of block_adapter past a group's count are ignored. An adapter may fill several blocks of a group. `adapter_home`: A permutation of the pool positions; position q is held by owner group q.
All inputs are finite; a program needn't handle non-finite values.
Results may differ from the reference program's by a relative error of at most 0.001.
Values may be sent and summed in bfloat16 or wider, within the bound.
No kernel may reach another device: no remote copies, remote signals or barrier semaphores. Data moves between devices by JAX's collectives and lax.ppermute only.
A program may use at most 64 MiB of HBM per device.

```python
import jax
import jax.numpy as jnp
from jax import lax

D = 8192
COLS = 512
R = 64
STEPS = 4
BLK = 112
CAP = 2
POOL = 8
TOTAL = 1792
N_GRP = 8


def draw_block_count(key, part):
    key = jax.random.fold_in(key, 11)
    key_counts, key_full = jax.random.split(key)
    counts = jax.random.randint(key_counts, (N_GRP,), 1, CAP + 1, dtype=jnp.int32)
    full_group = jax.random.randint(key_full, (), 0, N_GRP, dtype=jnp.int32)
    return counts.at[full_group].set(CAP)


def touch_ends(entries, own_key, least, high):
    extent = entries.shape
    index_at = [jax.random.randint(jax.random.fold_in(own_key, axis), (), 0, extent[axis]) for axis in range(len(extent))]
    entries = entries.at[tuple(index_at)].set(least)
    longest = extent.index(max(extent))
    index_at[longest] = (index_at[longest] + 1) % extent[longest]
    return entries.at[tuple(index_at)].set(high)


def levels(rng, extent, shards, least, top_value):
    def one(axis_at, blocks):
        steps = jax.random.uniform(jax.random.fold_in(jax.random.fold_in(rng, 6), axis_at), (blocks,), jnp.float32, least / len(shards), top_value / len(shards))
        return jnp.repeat(jnp.exp(steps), extent[axis_at] // blocks).reshape((-1,) + (1,) * (len(extent) - axis_at - 1))

    gain = one(*shards[0])
    for cut in shards[1:]:
        gain = gain * one(*cut)
    return gain


def gaussian(rng, shape, scale, most, shards=(), kind=jnp.bfloat16):
    drawn = jax.random.normal(rng, shape, jnp.float32) * scale
    if len(shards) > 0:
        drawn = levels(rng, shape, shards, -0.22, 0.18) * drawn
    return jnp.clip(drawn, min=-most, max=most).astype(kind)


def setup_inputs(seed: int = 0, part: int = 0) -> dict:
    arg_keys = jax.random.split(jax.random.key(seed), 8)
    part_keys = jax.random.split(jax.random.fold_in(arg_keys[7], part), 8)
    return {
        "hidden": gaussian(part_keys[0], (STEPS, TOTAL, D), 1.0, 6.0, ((1, 8), (2, 2))),
        "base_weight": gaussian(arg_keys[1], (D, COLS), D ** -0.5, 0.0625, ((0, 2),)),
        "pool_down": gaussian(arg_keys[2], (POOL, D, R), D ** -0.5, 0.0625, ((0, 8), (1, 2))),
        "pool_up": gaussian(arg_keys[3], (POOL, R, COLS), R ** -0.5, 0.75, ((0, 8),)),
        "adapter_home": jax.random.permutation(arg_keys[4], POOL).astype(jnp.int32),
        "block_adapter": touch_ends(jax.random.randint(part_keys[5], (N_GRP, CAP), 0, POOL), jax.random.fold_in(part_keys[5], 1), 0, POOL - 1).astype(jnp.int32),
        "block_count": draw_block_count(jax.random.fold_in(jax.random.fold_in(arg_keys[7], part), 71), part),
    }


adapter_scale_factor = 0.5


def reference(hidden, base_weight, pool_down, pool_up, adapter_home, block_adapter, block_count):
    position = adapter_home[block_adapter].astype(jnp.int32)
    live_slots = jnp.arange(CAP, dtype=jnp.int32)[None, :] < block_count[:, None]
    grouped = hidden.reshape(STEPS, N_GRP, CAP, BLK, D)
    grouped = jnp.transpose(grouped, (1, 0, 2, 3, 4))
    weight_wide = base_weight.astype(jnp.float32)

    def one_group(packed):
        rows_here, places, alive = packed
        rows_wide = rows_here.astype(jnp.float32)
        base_projection_output = jnp.einsum("scbd,dn->scbn", rows_wide, weight_wide, precision=lax.Precision.HIGHEST)
        down_sel = pool_down[places].astype(jnp.float32)
        selected_up_weight = pool_up[places].astype(jnp.float32)
        adapter_shrunk_rows = jnp.einsum("scbd,cdr->scbr", rows_wide, down_sel, precision=lax.Precision.HIGHEST)
        adapter_shrunk_rows = jnp.where(alive[None, :, None, None], adapter_shrunk_rows, jnp.float32(0.0))
        adapter_expanded_rows = jnp.einsum("scbr,crn->scbn", adapter_shrunk_rows, selected_up_weight, precision=lax.Precision.HIGHEST)
        return (base_projection_output + adapter_scale_factor * adapter_expanded_rows).astype(jnp.bfloat16)

    outputs = lax.map(one_group, (grouped, position, live_slots))
    outputs = jnp.transpose(outputs, (1, 0, 2, 3, 4))
    return outputs.reshape(STEPS, N_GRP * CAP * BLK, COLS)
```

```python
import functools

import jax
import jax.numpy as jnp
from jax import lax
from jax.experimental import pallas as pl
from jax.experimental.pallas import tpu as pltpu
from jax.sharding import PartitionSpec as P

adapter_scale_factor = 0.5
MEMBERS = 8
PIECE_ROWS = 16

ANY = pl.BlockSpec(memory_space=pl.ANY)
SMEM = pl.BlockSpec(memory_space=pltpu.SMEM)
VMEM = pl.BlockSpec(memory_space=pltpu.VMEM)


def pack_kernel(near, halves, down_ref, up_ref, *refs):
    outs, sem = refs[:near], refs[near]
    member_base = lax.axis_index("rep") * near
    low = lax.rem(lax.axis_index("grp"), near)
    tp_index = lax.axis_index("tp")
    wide = down_ref.shape[1] // halves
    up_own = up_ref.shape[1] // lax.axis_size("tp")
    up_wide = up_own // halves
    copies = []
    for flip in range(near):
        member = member_base + (low ^ flip)
        rows = pl.ds(pl.multiple_of(member // halves * PIECE_ROWS, PIECE_ROWS), PIECE_ROWS)
        half = lax.rem(member, halves)
        copies.append(
            pltpu.make_async_copy(
                down_ref.at[rows, pl.ds(pl.multiple_of(half * wide, 128), wide)],
                outs[flip].at[:, pl.ds(0, wide)],
                sem.at[2 * flip],
            )
        )
        copies.append(
            pltpu.make_async_copy(
                up_ref.at[
                    rows, pl.ds(pl.multiple_of(tp_index * up_own + half * up_wide, 128), up_wide)
                ],
                outs[flip].at[:, pl.ds(wide, up_wide)],
                sem.at[2 * flip + 1],
            )
        )
    for copy in copies:
        copy.start()
    for copy in copies:
        copy.wait()


def select_kernel(near, rep_count, part_count, home_ref, *refs):
    wanted, refs = refs[:rep_count], refs[rep_count:]
    held, refs = refs[:part_count], refs[part_count:]
    outs, sem = refs[: near * rep_count], refs[near * rep_count]
    group_index = lax.axis_index("grp")
    slot_count = outs[0].shape[0]
    depth = held[0].shape[0]
    pool_size = home_ref.shape[0]
    for flip in range(near * rep_count):
        other = group_index ^ (flip % near)
        for slot in range(slot_count):
            adapter = jnp.clip(wanted[flip // near][other, slot], 0, pool_size - 1)
            place = jnp.clip(home_ref[adapter], 0, pool_size - 1) ^ group_index
            for part in range(part_count):

                @pl.when(place // depth == part)
                def _():
                    pltpu.make_async_copy(
                        held[part].at[lax.rem(place, depth)],
                        outs[flip].at[slot],
                        sem.at[flip * slot_count + slot],
                    ).start()

    for flip in range(near * rep_count):
        for slot in range(slot_count):
            pltpu.make_async_copy(
                held[0].at[0], outs[flip].at[slot], sem.at[flip * slot_count + slot]
            ).wait()


def base_kernel(x_ref, weight_ref, mine_ref, theirs_ref):
    share = mine_ref.shape[2]
    product = jnp.dot(x_ref[0], weight_ref[...], preferred_element_type=jnp.float32)
    tp_index = lax.axis_index("tp")

    @pl.when(tp_index == 0)
    def _():
        mine_ref[0] = product[:, :share]
        theirs_ref[0] = product[:, share:]

    @pl.when(tp_index == 1)
    def _():
        mine_ref[0] = product[:, share:]
        theirs_ref[0] = product[:, :share]


def shrink_kernel(member_count, halves, rank, count_ref, x_ref, *refs):
    pieces, refs = refs[:member_count], refs[member_count:]
    shrunk_ref, up_ref, down = refs
    slot_count = pieces[0].shape[0]
    wide = down.shape[1] // halves
    up_wide = up_ref.shape[1] // halves
    group_index = lax.axis_index("grp")

    @pl.when(pl.program_id(0) == 0)
    def _():
        for flip in range(member_count):
            half = lax.rem(group_index ^ flip, halves)
            for slot in range(slot_count):
                rows = pl.ds(slot * rank + flip // halves * PIECE_ROWS, PIECE_ROWS)
                down[rows, pl.ds(pl.multiple_of(half * wide, 128), wide)] = pieces[flip][
                    slot, :, :wide
                ]
                up_ref[rows, pl.ds(pl.multiple_of(half * up_wide, 128), up_wide)] = pieces[flip][
                    slot, :, wide:
                ]

    product = lax.dot_general(
        x_ref[0], down[...], (((1,), (1,)), ((), ())), preferred_element_type=jnp.float32
    )
    rows = product.shape[0] // slot_count
    slot_of = lax.broadcasted_iota(jnp.int32, (rows, product.shape[1]), 1) // rank
    live_count = count_ref[group_index]
    packed = jnp.zeros((rows, product.shape[1]), jnp.float32)
    for slot in range(slot_count):
        keep = (slot_of == slot) & (slot < live_count)
        packed = jnp.where(keep, product[slot * rows : (slot + 1) * rows], packed)
    shrunk_ref[0] = packed


def expand_kernel(slot_count, rank, mine_ref, theirs_ref, up_ref, base_ref, out_ref):
    shrunk = mine_ref[0] + theirs_ref[0]
    rows = shrunk.shape[0]
    slot_of = lax.broadcasted_iota(jnp.int32, shrunk.shape, 1) // rank
    up = up_ref[...]
    top = shrunk.astype(jnp.bfloat16)
    rest = shrunk - top.astype(jnp.float32)
    mid = rest.astype(jnp.bfloat16)
    low = (rest - mid.astype(jnp.float32)).astype(jnp.bfloat16)
    up_thrice = jnp.concatenate([up, up, up], axis=0)
    for slot in range(slot_count):
        zero = jnp.zeros_like(top)
        terms = jnp.concatenate(
            [jnp.where(slot_of == slot, term, zero) for term in (top, mid, low)], axis=1
        )
        expanded = jnp.dot(terms, up_thrice, preferred_element_type=jnp.float32)
        at = pl.ds(slot * rows, rows)
        out_ref[0, at, :] = (base_ref[0, at, :] + adapter_scale_factor * expanded).astype(
            out_ref.dtype
        )


def local(hidden, base_weight, pool_down, pool_up, adapter_home, block_adapter, block_count):
    step_count, row_count, half_width = hidden.shape
    rep_count = lax.axis_size("rep")
    group_count = lax.axis_size("grp")
    rank = pool_up.shape[1]
    col_count = pool_up.shape[2]
    slot_count = block_adapter.shape[1]
    block_rows = row_count // slot_count
    share = col_count // lax.axis_size("tp")
    near = MEMBERS // rep_count
    halves = MEMBERS * PIECE_ROWS // rank
    piece_width = (half_width + share) // halves
    bf16, f32 = jnp.bfloat16, jnp.float32

    down = jnp.swapaxes(pool_down[0], 0, 1)
    pieces = pl.pallas_call(
        functools.partial(pack_kernel, near, halves),
        out_shape=[jax.ShapeDtypeStruct((PIECE_ROWS, piece_width), bf16)] * near,
        in_specs=[ANY, ANY],
        out_specs=[ANY] * near,
        scratch_shapes=[pltpu.SemaphoreType.DMA((2 * near,))],
        name="pack",
    )(down, pool_up[0])

    held = [pieces[0]] + [None] * (group_count - 1)
    for flip in sorted(range(1, group_count), key=lambda f: -f):
        pairs = [(g, g ^ flip) for g in range(group_count)]
        held[flip] = lax.ppermute(pieces[flip % near], "grp", pairs)
    wanted = [block_adapter]
    for flip in range(1, rep_count):
        pairs = [(r, r ^ flip) for r in range(rep_count)]
        wanted.append(lax.ppermute(block_adapter, "rep", pairs))
    if group_count <= MEMBERS:
        held = [piece[None] for piece in held]
    else:
        held = [jnp.stack(held)]

    mine, theirs = pl.pallas_call(
        base_kernel,
        grid=(step_count,),
        out_shape=[jax.ShapeDtypeStruct((step_count, row_count, share), f32)] * 2,
        in_specs=[
            pl.BlockSpec((1, row_count, half_width), lambda s: (s, 0, 0)),
            pl.BlockSpec((half_width, col_count), lambda s: (0, 0)),
        ],
        out_specs=[pl.BlockSpec((1, row_count, share), lambda s: (s, 0, 0))] * 2,
        compiler_params=pltpu.CompilerParams(vmem_limit_bytes=24 << 20),
        cost_estimate=pl.CostEstimate(
            flops=2 * step_count * row_count * half_width * col_count,
            bytes_accessed=2 * step_count * row_count * (half_width + 4 * share),
            transcendentals=0,
        ),
        name="base",
    )(hidden, base_weight)
    swap = [(0, 1), (1, 0)]
    base = mine + lax.ppermute(theirs, "tp", swap)

    sends = pl.pallas_call(
        functools.partial(select_kernel, near, rep_count, len(held)),
        out_shape=[jax.ShapeDtypeStruct((slot_count, PIECE_ROWS, piece_width), bf16)] * MEMBERS,
        in_specs=[SMEM] * (1 + rep_count) + [ANY] * len(held),
        out_specs=[ANY] * MEMBERS,
        scratch_shapes=[pltpu.SemaphoreType.DMA((MEMBERS * slot_count,))],
        name="select",
    )(adapter_home, *wanted, *held)
    got = [sends[0]] + [None] * (MEMBERS - 1)
    for flip in sorted(range(1, MEMBERS), key=lambda f: -f):
        pairs = [
            (r * group_count + g, (r ^ flip // near) * group_count + (g ^ flip % near))
            for r in range(rep_count)
            for g in range(group_count)
        ]
        got[flip] = lax.ppermute(sends[flip], ("rep", "grp"), pairs)

    both = slot_count * rank
    shrunk, up = pl.pallas_call(
        functools.partial(shrink_kernel, MEMBERS, halves, rank),
        grid=(step_count,),
        out_shape=[
            jax.ShapeDtypeStruct((step_count, block_rows, both), f32),
            jax.ShapeDtypeStruct((both, share), bf16),
        ],
        in_specs=[SMEM, pl.BlockSpec((1, row_count, half_width), lambda s: (s, 0, 0))]
        + [pl.BlockSpec((slot_count, PIECE_ROWS, piece_width), lambda s: (0, 0, 0))] * MEMBERS,
        out_specs=[
            pl.BlockSpec((1, block_rows, both), lambda s: (s, 0, 0)),
            pl.BlockSpec((both, share), lambda s: (0, 0)),
        ],
        scratch_shapes=[pltpu.VMEM((both, half_width), bf16)],
        compiler_params=pltpu.CompilerParams(vmem_limit_bytes=24 << 20),
        cost_estimate=pl.CostEstimate(
            flops=2 * step_count * row_count * half_width * both,
            bytes_accessed=2 * step_count * row_count * half_width,
            transcendentals=0,
        ),
        name="shrink",
    )(block_count, hidden, *got)
    shrunk_other = lax.ppermute(shrunk, "tp", swap)

    return pl.pallas_call(
        functools.partial(expand_kernel, slot_count, rank),
        grid=(step_count,),
        out_shape=jax.ShapeDtypeStruct((step_count, row_count, share), bf16),
        in_specs=[
            pl.BlockSpec((1, block_rows, both), lambda s: (s, 0, 0)),
            pl.BlockSpec((1, block_rows, both), lambda s: (s, 0, 0)),
            pl.BlockSpec((both, share), lambda s: (0, 0)),
            pl.BlockSpec((1, row_count, share), lambda s: (s, 0, 0)),
        ],
        out_specs=pl.BlockSpec((1, row_count, share), lambda s: (s, 0, 0)),
        name="expand",
    )(shrunk, shrunk_other, up, base)


def solution(mesh):
    in_specs = (
        P(None, ("rep", "grp"), "tp"),
        P("tp", None),
        P("grp", "tp", None),
        P("grp", None, None),
        P(),
        P("rep", None),
        P("rep"),
    )
    out_specs = P(None, ("rep", "grp"), "tp")
    return jax.shard_map(local, mesh=mesh, in_specs=in_specs, out_specs=out_specs, check_vma=False)
```

```python
import functools

import jax
import jax.numpy as jnp
from jax import lax
from jax.experimental import pallas as pl
from jax.experimental.pallas import tpu as pltpu
from jax.sharding import PartitionSpec as P

adapter_scale_factor = 0.5
MEMBERS = 8
PIECE_ROWS = 16

ANY = pl.BlockSpec(memory_space=pl.ANY)
SMEM = pl.BlockSpec(memory_space=pltpu.SMEM)
VMEM = pl.BlockSpec(memory_space=pltpu.VMEM)


def pack_kernel(near, halves, down_ref, up_ref, *outs):
    member_base = lax.axis_index("rep") * near
    low = lax.rem(lax.axis_index("grp"), near)
    tp_index = lax.axis_index("tp")
    wide = down_ref.shape[1] // halves
    up_own = up_ref.shape[1] // lax.axis_size("tp")
    up_wide = up_own // halves
    for flip in range(near):
        member = member_base + (low ^ flip)
        rows = pl.ds(pl.multiple_of(member // halves * PIECE_ROWS, PIECE_ROWS), PIECE_ROWS)
        half = lax.rem(member, halves)
        outs[flip][:, :wide] = down_ref[rows, pl.ds(pl.multiple_of(half * wide, 128), wide)]
        outs[flip][:, wide:] = up_ref[
            rows, pl.ds(pl.multiple_of(tp_index * up_own + half * up_wide, 128), up_wide)
        ]


def select_kernel(near, rep_count, part_count, home_ref, *refs):
    wanted, refs = refs[:rep_count], refs[rep_count:]
    held, refs = refs[:part_count], refs[part_count:]
    outs = refs[: near * rep_count]
    group_index = lax.axis_index("grp")
    slot_count = outs[0].shape[0]
    pool_size = home_ref.shape[0]
    if part_count == 1:
        stack = held[0]
    else:
        stack = refs[near * rep_count]
        for part in range(part_count):
            stack[part] = held[part][...]
    for flip in range(near * rep_count):
        other = group_index ^ (flip % near)
        for slot in range(slot_count):
            adapter = jnp.clip(wanted[flip // near][other, slot], 0, pool_size - 1)
            place = jnp.clip(home_ref[adapter], 0, pool_size - 1) ^ group_index
            outs[flip][slot] = stack[place]


def base_kernel(x_ref, weight_ref, mine_ref, theirs_ref):
    share = mine_ref.shape[2]
    tp_index = lax.axis_index("tp")
    for step in range(x_ref.shape[0]):
        product = jnp.dot(x_ref[step], weight_ref[...], preferred_element_type=jnp.float32)

        @pl.when(tp_index == 0)
        def _():
            mine_ref[step] = product[:, :share]
            theirs_ref[step] = product[:, share:]

        @pl.when(tp_index == 1)
        def _():
            mine_ref[step] = product[:, share:]
            theirs_ref[step] = product[:, :share]


def shrink_kernel(member_count, halves, rank, count_ref, x_ref, *refs):
    pieces, refs = refs[:member_count], refs[member_count:]
    shrunk_ref, up_ref, down = refs
    slot_count = pieces[0].shape[0]
    wide = down.shape[1] // halves
    up_wide = up_ref.shape[1] // halves
    group_index = lax.axis_index("grp")
    for flip in range(member_count):
        half = lax.rem(group_index ^ flip, halves)
        for slot in range(slot_count):
            rows = pl.ds(slot * rank + flip // halves * PIECE_ROWS, PIECE_ROWS)
            down[rows, pl.ds(pl.multiple_of(half * wide, 128), wide)] = pieces[flip][slot, :, :wide]
            up_ref[rows, pl.ds(pl.multiple_of(half * up_wide, 128), up_wide)] = pieces[flip][
                slot, :, wide:
            ]
    rows = shrunk_ref.shape[1]
    slot_of = lax.broadcasted_iota(jnp.int32, shrunk_ref.shape[1:], 1) // rank
    live_count = count_ref[group_index]
    for step in range(x_ref.shape[0]):
        product = lax.dot_general(
            x_ref[step], down[...], (((1,), (1,)), ((), ())), preferred_element_type=jnp.float32
        )
        packed = jnp.zeros(shrunk_ref.shape[1:], jnp.float32)
        for slot in range(slot_count):
            keep = (slot_of == slot) & (slot < live_count)
            packed = jnp.where(keep, product[slot * rows : (slot + 1) * rows], packed)
        shrunk_ref[step] = packed


def expand_kernel(
    slot_count, rank, mine_ref, theirs_ref, up_ref, base_ref, base_other_ref, out_ref, done, sem
):
    rows = mine_ref.shape[1]
    slot_of = lax.broadcasted_iota(jnp.int32, mine_ref.shape[1:], 1) // rank
    up = up_ref[...]
    up_thrice = jnp.concatenate([up, up, up], axis=0)
    for step in range(mine_ref.shape[0]):
        shrunk = mine_ref[step] + theirs_ref[step]
        top = shrunk.astype(jnp.bfloat16)
        rest = shrunk - top.astype(jnp.float32)
        mid = rest.astype(jnp.bfloat16)
        low = (rest - mid.astype(jnp.float32)).astype(jnp.bfloat16)
        zero = jnp.zeros_like(top)
        for slot in range(slot_count):
            terms = jnp.concatenate(
                [jnp.where(slot_of == slot, term, zero) for term in (top, mid, low)], axis=1
            )
            expanded = jnp.dot(terms, up_thrice, preferred_element_type=jnp.float32)
            at = pl.ds(slot * rows, rows)
            total = base_ref[step, at, :] + base_other_ref[step, at, :]
            done[step, at, :] = (total + adapter_scale_factor * expanded).astype(done.dtype)
        pltpu.make_async_copy(done.at[step], out_ref.at[step], sem.at[step]).start()
    for step in range(mine_ref.shape[0]):
        pltpu.make_async_copy(done.at[step], out_ref.at[step], sem.at[step]).wait()


def local(hidden, base_weight, pool_down, pool_up, adapter_home, block_adapter, block_count):
    step_count, row_count, half_width = hidden.shape
    rep_count = lax.axis_size("rep")
    group_count = lax.axis_size("grp")
    rank = pool_up.shape[1]
    col_count = pool_up.shape[2]
    slot_count = block_adapter.shape[1]
    block_rows = row_count // slot_count
    share = col_count // lax.axis_size("tp")
    near = MEMBERS // rep_count
    halves = MEMBERS * PIECE_ROWS // rank
    piece_width = (half_width + share) // halves
    bf16, f32 = jnp.bfloat16, jnp.float32

    down = jnp.swapaxes(pool_down[0], 0, 1)
    pieces = pl.pallas_call(
        functools.partial(pack_kernel, near, halves),
        out_shape=[jax.ShapeDtypeStruct((PIECE_ROWS, piece_width), bf16)] * near,
        in_specs=[VMEM, VMEM],
        out_specs=[VMEM] * near,
        name="pack",
    )(down, pool_up[0])

    held = [pieces[0]] + [None] * (group_count - 1)
    for flip in range(group_count - 1, 0, -1):
        pairs = [(g, g ^ flip) for g in range(group_count)]
        held[flip] = lax.ppermute(pieces[flip % near], "grp", pairs)
    wanted = [block_adapter]
    for flip in range(1, rep_count):
        pairs = [(r, r ^ flip) for r in range(rep_count)]
        wanted.append(lax.ppermute(block_adapter, "rep", pairs))

    mine, theirs = pl.pallas_call(
        base_kernel,
        out_shape=[jax.ShapeDtypeStruct((step_count, row_count, share), f32)] * 2,
        in_specs=[VMEM, VMEM],
        out_specs=[VMEM, VMEM],
        compiler_params=pltpu.CompilerParams(vmem_limit_bytes=24 << 20),
        cost_estimate=pl.CostEstimate(
            flops=2 * step_count * row_count * half_width * col_count,
            bytes_accessed=2 * step_count * row_count * (half_width + 4 * share),
            transcendentals=0,
        ),
        name="base",
    )(hidden, base_weight)
    held[1:], wanted[1:], mine, theirs = lax.optimization_barrier(
        (held[1:], wanted[1:], mine, theirs)
    )

    if group_count <= MEMBERS:
        parts = held
        stack = [pltpu.VMEM((group_count, PIECE_ROWS, piece_width), bf16)]
    else:
        parts, stack = [jnp.stack(held)], []
    sends = pl.pallas_call(
        functools.partial(select_kernel, near, rep_count, len(parts)),
        out_shape=[jax.ShapeDtypeStruct((slot_count, PIECE_ROWS, piece_width), bf16)] * MEMBERS,
        in_specs=[SMEM] * (1 + rep_count) + [VMEM] * len(parts),
        out_specs=[VMEM] * MEMBERS,
        scratch_shapes=stack,
        compiler_params=pltpu.CompilerParams(vmem_limit_bytes=24 << 20),
        name="select",
    )(adapter_home, *wanted, *parts)
    swap = [(0, 1), (1, 0)]
    theirs, sends = lax.optimization_barrier((theirs, sends))
    base_other = lax.ppermute(theirs, "tp", swap)
    got = [sends[0]] + [None] * (MEMBERS - 1)
    for flip in range(MEMBERS - 1, 0, -1):
        pairs = [
            (r * group_count + g, (r ^ flip // near) * group_count + (g ^ flip % near))
            for r in range(rep_count)
            for g in range(group_count)
        ]
        got[flip] = lax.ppermute(sends[flip], ("rep", "grp"), pairs)

    both = slot_count * rank
    shrunk, up = pl.pallas_call(
        functools.partial(shrink_kernel, MEMBERS, halves, rank),
        out_shape=[
            jax.ShapeDtypeStruct((step_count, block_rows, both), f32),
            jax.ShapeDtypeStruct((both, share), bf16),
        ],
        in_specs=[SMEM] + [VMEM] * (1 + MEMBERS),
        out_specs=[VMEM, VMEM],
        scratch_shapes=[pltpu.VMEM((both, half_width), bf16)],
        compiler_params=pltpu.CompilerParams(vmem_limit_bytes=24 << 20),
        cost_estimate=pl.CostEstimate(
            flops=2 * step_count * row_count * half_width * both,
            bytes_accessed=2 * step_count * row_count * half_width,
            transcendentals=0,
        ),
        name="shrink",
    )(block_count, hidden, *got)
    shrunk_other = lax.ppermute(shrunk, "tp", swap)

    return pl.pallas_call(
        functools.partial(expand_kernel, slot_count, rank),
        out_shape=jax.ShapeDtypeStruct((step_count, row_count, share), bf16),
        in_specs=[VMEM] * 5,
        out_specs=ANY,
        scratch_shapes=[
            pltpu.VMEM((step_count, row_count, share), bf16),
            pltpu.SemaphoreType.DMA((step_count,)),
        ],
        compiler_params=pltpu.CompilerParams(vmem_limit_bytes=24 << 20),
        name="expand",
    )(shrunk, shrunk_other, up, mine, base_other)


def solution(mesh):
    in_specs = (
        P(None, ("rep", "grp"), "tp"),
        P("tp", None),
        P("grp", "tp", None),
        P("grp", None, None),
        P(),
        P("rep", None),
        P("rep"),
    )
    out_specs = P(None, ("rep", "grp"), "tp")
    return jax.shard_map(local, mesh=mesh, in_specs=in_specs, out_specs=out_specs, check_vma=False)
```

```python
import functools

import jax
import jax.numpy as jnp
from jax import lax
from jax.experimental import pallas as pl
from jax.experimental.pallas import tpu as pltpu
from jax.sharding import PartitionSpec as P

adapter_scale_factor = 0.5
MEMBERS = 8
PIECE_ROWS = 16

ANY = pl.BlockSpec(memory_space=pl.ANY)
SMEM = pl.BlockSpec(memory_space=pltpu.SMEM)
VMEM = pl.BlockSpec(memory_space=pltpu.VMEM)


def pack_kernel(near, halves, down_ref, up_ref, *refs):
    outs, sem = refs[:-1], refs[-1]
    member_base = lax.axis_index("rep") * near
    low = lax.rem(lax.axis_index("grp"), near)
    tp_index = lax.axis_index("tp")
    wide = down_ref.shape[1] // halves
    up_own = up_ref.shape[1] // lax.axis_size("tp")
    up_wide = up_own // halves
    copies = []
    for at, out in enumerate(outs):
        member = member_base + (low ^ at % near)
        rows = pl.ds(pl.multiple_of(member // halves * PIECE_ROWS, PIECE_ROWS), PIECE_ROWS)
        half = lax.rem(member, halves)
        down_at = pl.ds(pl.multiple_of(half * wide, 128), wide)
        up_at = pl.ds(pl.multiple_of(tp_index * up_own + half * up_wide, 128), up_wide)
        copies += [
            pltpu.make_async_copy(
                down_ref.at[rows, down_at], out.at[:, pl.ds(0, wide)], sem.at[2 * at]
            ),
            pltpu.make_async_copy(
                up_ref.at[rows, up_at], out.at[:, pl.ds(wide, up_wide)], sem.at[2 * at + 1]
            ),
        ]
    for copy in copies:
        copy.start()
    for copy in copies:
        copy.wait()


def select_kernel(near, rep_count, part_count, home_ref, *refs):
    wanted, refs = refs[:rep_count], refs[rep_count:]
    held, refs = refs[:part_count], refs[part_count:]
    outs = refs[: near * rep_count]
    group_index = lax.axis_index("grp")
    slot_count = outs[0].shape[0]
    pool_size = home_ref.shape[0]
    if part_count == 1:
        stack = held[0]
    else:
        stack = refs[near * rep_count]
        for part in range(part_count):
            stack[part_count - 1 - part] = held[part][...]
    for flip in range(near * rep_count):
        other = group_index ^ (flip % near)
        for slot in range(slot_count):
            adapter = jnp.clip(wanted[flip // near][slot, other], 0, pool_size - 1)
            place = jnp.clip(home_ref[adapter], 0, pool_size - 1) ^ group_index
            outs[flip][slot] = stack[place]


def base_kernel(x_ref, weight_ref, mine_ref, theirs_ref):
    rows, share = mine_ref.shape
    x = x_ref[...].reshape(rows, x_ref.shape[2])
    product = jnp.dot(x, weight_ref[...], preferred_element_type=jnp.float32)
    first, second = product[:, :share], product[:, share:]
    tp_index = lax.axis_index("tp")
    fresh = pl.program_id(0) == 0

    def store(mine, theirs):
        @pl.when(fresh)
        def _():
            mine_ref[...] = mine
            theirs_ref[...] = theirs

        @pl.when(jnp.logical_not(fresh))
        def _():
            mine_ref[...] += mine
            theirs_ref[...] += theirs

    @pl.when(tp_index == 0)
    def _():
        store(first, second)

    @pl.when(tp_index == 1)
    def _():
        store(second, first)


def shrink_kernel(member_count, halves, rank, count_ref, x_ref, *refs):
    pieces, refs = refs[:member_count][::-1], refs[member_count:]
    shrunk_ref, up_ref, down = refs
    slot_count = pieces[0].shape[0]
    wide = down.shape[1] // halves
    up_wide = up_ref.shape[1] // halves
    group_index = lax.axis_index("grp")
    for flip in range(member_count):
        half = lax.rem(group_index ^ flip, halves)
        for slot in range(slot_count):
            rows = pl.ds(slot * rank + flip // halves * PIECE_ROWS, PIECE_ROWS)
            down[rows, pl.ds(pl.multiple_of(half * wide, 128), wide)] = pieces[flip][slot, :, :wide]
            up_ref[rows, pl.ds(pl.multiple_of(half * up_wide, 128), up_wide)] = pieces[flip][
                slot, :, wide:
            ]
    rows = shrunk_ref.shape[1]
    slot_of = lax.broadcasted_iota(jnp.int32, shrunk_ref.shape[1:], 1) // rank
    live_count = count_ref[group_index]
    for step in range(x_ref.shape[0]):
        product = lax.dot_general(
            x_ref[step], down[...], (((1,), (1,)), ((), ())), preferred_element_type=jnp.float32
        )
        packed = jnp.zeros(shrunk_ref.shape[1:], jnp.float32)
        for slot in range(slot_count):
            keep = (slot_of == slot) & (slot < live_count)
            packed = jnp.where(keep, product[slot * rows : (slot + 1) * rows], packed)
        shrunk_ref[step] = packed


def expand_kernel(
    slot_count, rank, mine_ref, theirs_ref, up_ref, base_ref, base_other_ref, out_ref, done, sem
):
    rows = mine_ref.shape[1]
    slot_of = lax.broadcasted_iota(jnp.int32, mine_ref.shape[1:], 1) // rank
    up = up_ref[...]
    up_thrice = jnp.concatenate([up, up, up], axis=0)
    for step in range(mine_ref.shape[0]):
        shrunk = mine_ref[step] + theirs_ref[step]
        top = shrunk.astype(jnp.bfloat16)
        rest = shrunk - top.astype(jnp.float32)
        mid = rest.astype(jnp.bfloat16)
        low = (rest - mid.astype(jnp.float32)).astype(jnp.bfloat16)
        zero = jnp.zeros_like(top)
        for slot in range(slot_count):
            terms = jnp.concatenate(
                [jnp.where(slot_of == slot, term, zero) for term in (top, mid, low)], axis=1
            )
            expanded = jnp.dot(terms, up_thrice, preferred_element_type=jnp.float32)
            at = pl.ds((step * slot_count + slot) * rows, rows)
            total = base_ref[at, :] + base_other_ref[at, :]
            done[step, pl.ds(slot * rows, rows), :] = (total + adapter_scale_factor * expanded).astype(done.dtype)
        pltpu.make_async_copy(done.at[step], out_ref.at[step], sem.at[step]).start()
    for step in range(mine_ref.shape[0]):
        pltpu.make_async_copy(done.at[step], out_ref.at[step], sem.at[step]).wait()


def local(hidden, base_weight, pool_down, pool_up, adapter_home, block_adapter, block_count):
    step_count, row_count, half_width = hidden.shape
    rep_count = lax.axis_size("rep")
    group_count = lax.axis_size("grp")
    rank = pool_up.shape[1]
    col_count = pool_up.shape[2]
    slot_count = block_adapter.shape[1]
    block_rows = row_count // slot_count
    share = col_count // lax.axis_size("tp")
    near = MEMBERS // rep_count
    halves = MEMBERS * PIECE_ROWS // rank
    piece_width = (half_width + share) // halves
    bf16, f32 = jnp.bfloat16, jnp.float32

    down = jnp.swapaxes(pool_down[0], 0, 1)
    distinct = group_count if group_count <= MEMBERS else near
    pieces = pl.pallas_call(
        functools.partial(pack_kernel, near, halves),
        out_shape=[jax.ShapeDtypeStruct((PIECE_ROWS, piece_width), bf16)] * distinct,
        in_specs=[ANY, ANY],
        out_specs=[VMEM] * distinct,
        scratch_shapes=[pltpu.SemaphoreType.DMA((2 * distinct,))],
        compiler_params=pltpu.CompilerParams(vmem_limit_bytes=56 << 20),
        name="pack",
    )(down, pool_up[0])

    held = [pieces[0]] + [None] * (group_count - 1)
    for flip in range(group_count - 1, 0, -1):
        pairs = [(g, g ^ flip) for g in range(group_count)]
        held[flip] = lax.ppermute(pieces[flip % distinct], "grp", pairs)
    asked = jnp.swapaxes(block_adapter, 0, 1)
    wanted = [asked]
    for flip in range(1, rep_count):
        pairs = [(r, r ^ flip) for r in range(rep_count)]
        wanted.append(lax.ppermute(asked, "rep", pairs))

    chunk_count = 4
    chunk = half_width // chunk_count
    rows = step_count * row_count
    mine, theirs = pl.pallas_call(
        base_kernel,
        grid=(chunk_count,),
        out_shape=[jax.ShapeDtypeStruct((rows, share), f32)] * 2,
        in_specs=[
            pl.BlockSpec((step_count, row_count, chunk), lambda k: (0, 0, k)),
            pl.BlockSpec((chunk, col_count), lambda k: (k, 0)),
        ],
        out_specs=[pl.BlockSpec((rows, share), lambda k: (0, 0))] * 2,
        compiler_params=pltpu.CompilerParams(vmem_limit_bytes=52 << 20),
        cost_estimate=pl.CostEstimate(
            flops=2 * rows * half_width * col_count,
            bytes_accessed=2 * rows * (half_width + 4 * share),
            transcendentals=0,
        ),
        name="base",
    )(hidden, base_weight)
    held[1:], wanted[1:], mine, theirs = lax.optimization_barrier(
        (held[1:], wanted[1:], mine, theirs)
    )

    if group_count <= MEMBERS:
        parts = held[::-1]
        stack = [pltpu.VMEM((group_count, PIECE_ROWS, piece_width), bf16)]
    else:
        parts, stack = [jnp.stack(held)], []
    sends = pl.pallas_call(
        functools.partial(select_kernel, near, rep_count, len(parts)),
        out_shape=[jax.ShapeDtypeStruct((slot_count, PIECE_ROWS, piece_width), bf16)] * MEMBERS,
        in_specs=[SMEM] * (1 + rep_count) + [VMEM] * len(parts),
        out_specs=[VMEM] * MEMBERS,
        scratch_shapes=stack,
        compiler_params=pltpu.CompilerParams(vmem_limit_bytes=24 << 20),
        name="select",
    )(adapter_home, *wanted, *parts)
    swap = [(0, 1), (1, 0)]
    theirs, sends = lax.optimization_barrier((theirs, sends))
    base_other = lax.ppermute(theirs, "tp", swap)
    got = [sends[0]] + [None] * (MEMBERS - 1)
    for flip in range(MEMBERS - 1, 0, -1):
        pairs = [
            (r * group_count + g, (r ^ flip // near) * group_count + (g ^ flip % near))
            for r in range(rep_count)
            for g in range(group_count)
        ]
        got[flip] = lax.ppermute(sends[flip], ("rep", "grp"), pairs)

    both = slot_count * rank
    shrunk, up = pl.pallas_call(
        functools.partial(shrink_kernel, MEMBERS, halves, rank),
        out_shape=[
            jax.ShapeDtypeStruct((step_count, block_rows, both), f32),
            jax.ShapeDtypeStruct((both, share), bf16),
        ],
        in_specs=[SMEM] + [VMEM] * (1 + MEMBERS),
        out_specs=[VMEM, VMEM],
        scratch_shapes=[pltpu.VMEM((both, half_width), bf16)],
        compiler_params=pltpu.CompilerParams(vmem_limit_bytes=24 << 20),
        cost_estimate=pl.CostEstimate(
            flops=2 * step_count * row_count * half_width * both,
            bytes_accessed=2 * step_count * row_count * half_width,
            transcendentals=0,
        ),
        name="shrink",
    )(block_count, hidden, *got[::-1])
    shrunk_other = lax.ppermute(shrunk, "tp", swap)

    return pl.pallas_call(
        functools.partial(expand_kernel, slot_count, rank),
        out_shape=jax.ShapeDtypeStruct((step_count, row_count, share), bf16),
        in_specs=[VMEM] * 5,
        out_specs=ANY,
        scratch_shapes=[
            pltpu.VMEM((step_count, row_count, share), bf16),
            pltpu.SemaphoreType.DMA((step_count,)),
        ],
        compiler_params=pltpu.CompilerParams(vmem_limit_bytes=24 << 20),
        name="expand",
    )(shrunk, shrunk_other, up, mine, base_other)


def solution(mesh):
    in_specs = (
        P(None, ("rep", "grp"), "tp"),
        P("tp", None),
        P("grp", "tp", None),
        P("grp", None, None),
        P(),
        P("rep", None),
        P("rep"),
    )
    out_specs = P(None, ("rep", "grp"), "tp")
    return jax.shard_map(local, mesh=mesh, in_specs=in_specs, out_specs=out_specs, check_vma=False)
```

```python
import functools

import jax
import jax.numpy as jnp
from jax import lax
from jax.experimental import pallas as pl
from jax.experimental.pallas import tpu as pltpu
from jax.sharding import PartitionSpec as P

adapter_scale_factor = 0.5
MEMBERS = 8
PIECE_ROWS = 16
ORDER = (1, 7, 2, 4, 3, 5, 6)

ANY = pl.BlockSpec(memory_space=pl.ANY)
SMEM = pl.BlockSpec(memory_space=pltpu.SMEM)
VMEM = pl.BlockSpec(memory_space=pltpu.VMEM)


def pack_kernel(near, halves, down_ref, up_ref, out_ref, sem):
    member_base = lax.axis_index("rep") * near
    tp_index = lax.axis_index("tp")
    wide = down_ref.shape[1] // halves
    up_own = up_ref.shape[1] // lax.axis_size("tp")
    up_wide = up_own // halves
    copies = []
    for group in range(out_ref.shape[0]):
        member = member_base + group % near
        rows = pl.ds(pl.multiple_of(member // halves * PIECE_ROWS, PIECE_ROWS), PIECE_ROWS)
        half = lax.rem(member, halves)
        down_at = pl.ds(pl.multiple_of(half * wide, 128), wide)
        up_at = pl.ds(pl.multiple_of(tp_index * up_own + half * up_wide, 128), up_wide)
        copies += [
            pltpu.make_async_copy(
                down_ref.at[rows, down_at], out_ref.at[group, :, pl.ds(0, wide)], sem.at[2 * group]
            ),
            pltpu.make_async_copy(
                up_ref.at[rows, up_at],
                out_ref.at[group, :, pl.ds(wide, up_wide)],
                sem.at[2 * group + 1],
            ),
        ]
    for copy in copies:
        copy.start()
    for copy in copies:
        copy.wait()


def select_kernel(near, rep_count, home_ref, *refs):
    wanted, held_ref, outs = refs[:rep_count], refs[rep_count], refs[rep_count + 1 :]
    group_index = lax.axis_index("grp")
    pool_size = home_ref.shape[0]
    for flip, out in zip((0,) + ORDER, outs):
        other = group_index ^ (flip % near)
        for slot in range(out.shape[0]):
            adapter = jnp.clip(wanted[flip // near][slot, other], 0, pool_size - 1)
            place = jnp.clip(home_ref[adapter], 0, pool_size - 1)
            out[slot] = held_ref[place]


def stage_kernel(x_ref, out_ref, sem):
    copy = pltpu.make_async_copy(x_ref, out_ref, sem)
    copy.start()
    copy.wait()


def base_kernel(x_ref, weight_ref, mine_ref, theirs_ref):
    rows, share = mine_ref.shape
    x = x_ref[...].reshape(rows, x_ref.shape[2])
    product = jnp.dot(x, weight_ref[...], preferred_element_type=jnp.float32)
    first, second = product[:, :share], product[:, share:]
    tp_index = lax.axis_index("tp")
    fresh = pl.program_id(0) == 0

    def store(mine, theirs):
        @pl.when(fresh)
        def _():
            mine_ref[...] = mine
            theirs_ref[...] = theirs

        @pl.when(jnp.logical_not(fresh))
        def _():
            mine_ref[...] += mine
            theirs_ref[...] += theirs

    @pl.when(tp_index == 0)
    def _():
        store(first, second)

    @pl.when(tp_index == 1)
    def _():
        store(second, first)


def shrink_kernel(halves, rank, count_ref, x_ref, *refs):
    pieces, (shrunk_ref, up_ref, down) = refs[:-3], refs[-3:]
    slot_count = pieces[0].shape[0]
    wide = down.shape[1] // halves
    up_wide = up_ref.shape[1] // halves
    group_index = lax.axis_index("grp")
    for flip, piece in zip((0,) + ORDER, pieces):
        half = lax.rem(group_index ^ flip, halves)
        for slot in range(slot_count):
            rows = pl.ds(slot * rank + flip // halves * PIECE_ROWS, PIECE_ROWS)
            down[rows, pl.ds(pl.multiple_of(half * wide, 128), wide)] = piece[slot, :, :wide]
            up_ref[rows, pl.ds(pl.multiple_of(half * up_wide, 128), up_wide)] = piece[
                slot, :, wide:
            ]
    rows = shrunk_ref.shape[1]
    slot_of = lax.broadcasted_iota(jnp.int32, shrunk_ref.shape[1:], 1) // rank
    live_count = count_ref[group_index]
    for step in range(x_ref.shape[0]):
        product = lax.dot_general(
            x_ref[step], down[...], (((1,), (1,)), ((), ())), preferred_element_type=jnp.float32
        )
        packed = jnp.zeros(shrunk_ref.shape[1:], jnp.float32)
        for slot in range(slot_count):
            keep = (slot_of == slot) & (slot < live_count)
            packed = jnp.where(keep, product[slot * rows : (slot + 1) * rows], packed)
        shrunk_ref[step] = packed


def expand_kernel(
    slot_count, rank, mine_ref, theirs_ref, up_ref, base_ref, base_other_ref, out_ref, done, sem
):
    rows = mine_ref.shape[1]
    slot_of = lax.broadcasted_iota(jnp.int32, mine_ref.shape[1:], 1) // rank
    up = up_ref[...]
    up_thrice = jnp.concatenate([up, up, up], axis=0)
    for step in range(mine_ref.shape[0]):
        shrunk = mine_ref[step] + theirs_ref[step]
        top = shrunk.astype(jnp.bfloat16)
        rest = shrunk - top.astype(jnp.float32)
        mid = rest.astype(jnp.bfloat16)
        low = (rest - mid.astype(jnp.float32)).astype(jnp.bfloat16)
        zero = jnp.zeros_like(top)
        for slot in range(slot_count):
            terms = jnp.concatenate(
                [jnp.where(slot_of == slot, term, zero) for term in (top, mid, low)], axis=1
            )
            expanded = jnp.dot(terms, up_thrice, preferred_element_type=jnp.float32)
            at = pl.ds((step * slot_count + slot) * rows, rows)
            total = base_ref[at, :] + base_other_ref[at, :]
            done[step, pl.ds(slot * rows, rows), :] = (total + adapter_scale_factor * expanded).astype(done.dtype)
        pltpu.make_async_copy(done.at[step], out_ref.at[step], sem.at[step]).start()
    for step in range(mine_ref.shape[0]):
        pltpu.make_async_copy(done.at[step], out_ref.at[step], sem.at[step]).wait()


def local(hidden, base_weight, pool_down, pool_up, adapter_home, block_adapter, block_count):
    step_count, row_count, half_width = hidden.shape
    rep_count = lax.axis_size("rep")
    group_count = lax.axis_size("grp")
    rank = pool_up.shape[1]
    col_count = pool_up.shape[2]
    slot_count = block_adapter.shape[1]
    block_rows = row_count // slot_count
    share = col_count // lax.axis_size("tp")
    near = MEMBERS // rep_count
    halves = MEMBERS * PIECE_ROWS // rank
    piece_width = (half_width + share) // halves
    bf16, f32 = jnp.bfloat16, jnp.float32

    down = jnp.swapaxes(pool_down[0], 0, 1)
    packed = pl.pallas_call(
        functools.partial(pack_kernel, near, halves),
        out_shape=jax.ShapeDtypeStruct((group_count, PIECE_ROWS, piece_width), bf16),
        in_specs=[ANY, ANY],
        out_specs=VMEM,
        scratch_shapes=[pltpu.SemaphoreType.DMA((2 * group_count,))],
        compiler_params=pltpu.CompilerParams(vmem_limit_bytes=56 << 20),
        name="pack",
    )(down, pool_up[0])
    held = lax.all_to_all(packed, "grp", 0, 0, tiled=True)
    asked = jnp.swapaxes(block_adapter, 0, 1)
    wanted = [asked]
    for flip in range(1, rep_count):
        pairs = [(r, r ^ flip) for r in range(rep_count)]
        wanted.append(lax.ppermute(asked, "rep", pairs))

    near_hidden = pl.pallas_call(
        stage_kernel,
        out_shape=pltpu.VMEM(hidden.shape, bf16),
        in_specs=[ANY],
        out_specs=VMEM,
        scratch_shapes=[pltpu.SemaphoreType.DMA(())],
        compiler_params=pltpu.CompilerParams(vmem_limit_bytes=40 << 20),
        cost_estimate=pl.CostEstimate(
            flops=0, bytes_accessed=4 * hidden.size, transcendentals=0
        ),
        name="stage",
    )(hidden)
    chunk_count = 4
    chunk = half_width // chunk_count
    rows = step_count * row_count
    mine, theirs = pl.pallas_call(
        base_kernel,
        grid=(chunk_count,),
        out_shape=[jax.ShapeDtypeStruct((rows, share), f32)] * 2,
        in_specs=[
            pl.BlockSpec((step_count, row_count, chunk), lambda k: (0, 0, k)),
            pl.BlockSpec((chunk, col_count), lambda k: (k, 0)),
        ],
        out_specs=[pl.BlockSpec((rows, share), lambda k: (0, 0))] * 2,
        compiler_params=pltpu.CompilerParams(vmem_limit_bytes=40 << 20),
        cost_estimate=pl.CostEstimate(
            flops=2 * rows * half_width * col_count,
            bytes_accessed=2 * rows * (half_width + 4 * share),
            transcendentals=0,
        ),
        name="base",
    )(near_hidden, base_weight)
    swap = [(0, 1), (1, 0)]
    base_other = lax.ppermute(theirs, "tp", swap)
    held, wanted[1:], mine, base_other = lax.optimization_barrier(
        (held, wanted[1:], mine, base_other)
    )

    sends = pl.pallas_call(
        functools.partial(select_kernel, near, rep_count),
        out_shape=[jax.ShapeDtypeStruct((slot_count, PIECE_ROWS, piece_width), bf16)] * MEMBERS,
        in_specs=[SMEM] * (1 + rep_count) + [VMEM],
        out_specs=[VMEM] * MEMBERS,
        compiler_params=pltpu.CompilerParams(vmem_limit_bytes=12 << 20),
        name="select",
    )(adapter_home, *wanted, held)
    got = []
    for flip, send in zip(ORDER, sends[1:]):
        pairs = [
            (r * group_count + g, (r ^ flip // near) * group_count + (g ^ flip % near))
            for r in range(rep_count)
            for g in range(group_count)
        ]
        got.append(lax.ppermute(send, ("rep", "grp"), pairs))

    both = slot_count * rank
    shrunk, up = pl.pallas_call(
        functools.partial(shrink_kernel, halves, rank),
        out_shape=[
            jax.ShapeDtypeStruct((step_count, block_rows, both), f32),
            jax.ShapeDtypeStruct((both, share), bf16),
        ],
        in_specs=[SMEM] + [VMEM] * (1 + MEMBERS),
        out_specs=[VMEM, VMEM],
        scratch_shapes=[pltpu.VMEM((both, half_width), bf16)],
        compiler_params=pltpu.CompilerParams(vmem_limit_bytes=12 << 20),
        cost_estimate=pl.CostEstimate(
            flops=2 * rows * half_width * both,
            bytes_accessed=2 * rows * half_width,
            transcendentals=0,
        ),
        name="shrink",
    )(block_count, near_hidden, sends[0], *got)
    shrunk_other = lax.ppermute(shrunk, "tp", swap)

    return pl.pallas_call(
        functools.partial(expand_kernel, slot_count, rank),
        out_shape=jax.ShapeDtypeStruct((step_count, row_count, share), bf16),
        in_specs=[VMEM] * 5,
        out_specs=ANY,
        scratch_shapes=[
            pltpu.VMEM((step_count, row_count, share), bf16),
            pltpu.SemaphoreType.DMA((step_count,)),
        ],
        compiler_params=pltpu.CompilerParams(vmem_limit_bytes=12 << 20),
        name="expand",
    )(shrunk, shrunk_other, up, mine, base_other)


def solution(mesh):
    in_specs = (
        P(None, ("rep", "grp"), "tp"),
        P("tp", None),
        P("grp", "tp", None),
        P("grp", None, None),
        P(),
        P("rep", None),
        P("rep"),
    )
    out_specs = P(None, ("rep", "grp"), "tp")
    return jax.shard_map(local, mesh=mesh, in_specs=in_specs, out_specs=out_specs, check_vma=False)
```

```python
import functools

import jax
import jax.numpy as jnp
from jax import lax
from jax.experimental import pallas as pl
from jax.experimental.pallas import tpu as pltpu
from jax.sharding import PartitionSpec as P

adapter_scale_factor = 0.5
MEMBERS = 8
PIECE_ROWS = 16
ORDER = (1, 7, 2, 4, 3, 5, 6)

ANY = pl.BlockSpec(memory_space=pl.ANY)
SMEM = pl.BlockSpec(memory_space=pltpu.SMEM)
VMEM = pl.BlockSpec(memory_space=pltpu.VMEM)


def pack_kernel(near, halves, down_ref, up_ref, out_ref, sem):
    member_base = lax.axis_index("rep") * near
    tp_index = lax.axis_index("tp")
    wide = down_ref.shape[1] // halves
    up_own = up_ref.shape[1] // lax.axis_size("tp")
    up_wide = up_own // halves
    copies = []
    for group in range(out_ref.shape[0]):
        member = member_base + group % near
        rows = pl.ds(pl.multiple_of(member // halves * PIECE_ROWS, PIECE_ROWS), PIECE_ROWS)
        half = lax.rem(member, halves)
        down_at = pl.ds(pl.multiple_of(half * wide, 128), wide)
        up_at = pl.ds(pl.multiple_of(tp_index * up_own + half * up_wide, 128), up_wide)
        copies += [
            pltpu.make_async_copy(
                down_ref.at[rows, down_at], out_ref.at[group, :, pl.ds(0, wide)], sem.at[2 * group]
            ),
            pltpu.make_async_copy(
                up_ref.at[rows, up_at],
                out_ref.at[group, :, pl.ds(wide, up_wide)],
                sem.at[2 * group + 1],
            ),
        ]
    for copy in copies:
        copy.start()
    for copy in copies:
        copy.wait()


def select_kernel(near, rep_count, home_ref, *refs):
    wanted, held_ref, outs = refs[:rep_count], refs[rep_count], refs[rep_count + 1 :]
    group_index = lax.axis_index("grp")
    pool_size = home_ref.shape[0]
    for flip, out in zip((0,) + ORDER, outs):
        other = group_index ^ (flip % near)
        for slot in range(out.shape[0]):
            adapter = jnp.clip(wanted[flip // near][slot, other], 0, pool_size - 1)
            place = jnp.clip(home_ref[adapter], 0, pool_size - 1)
            out[slot] = held_ref[place]


def stage_kernel(x_ref, out_ref, sem):
    copy = pltpu.make_async_copy(x_ref, out_ref, sem)
    copy.start()
    copy.wait()


def base_kernel(x_ref, weight_ref, mine_ref, theirs_ref):
    rows, share = mine_ref.shape
    x = x_ref[...].reshape(rows, x_ref.shape[2])
    product = jnp.dot(x, weight_ref[...], preferred_element_type=jnp.float32)
    first, second = product[:, :share], product[:, share:]
    tp_index = lax.axis_index("tp")
    fresh = pl.program_id(0) == 0

    def store(mine, theirs):
        @pl.when(fresh)
        def _():
            mine_ref[...] = mine
            theirs_ref[...] = theirs

        @pl.when(jnp.logical_not(fresh))
        def _():
            mine_ref[...] += mine
            theirs_ref[...] += theirs

    @pl.when(tp_index == 0)
    def _():
        store(first, second)

    @pl.when(tp_index == 1)
    def _():
        store(second, first)


def shrink_kernel(halves, rank, count_ref, x_ref, *refs):
    pieces, (shrunk_ref, up_ref, down) = refs[:-3], refs[-3:]
    slot_count = pieces[0].shape[0]
    wide = down.shape[1] // halves
    up_wide = up_ref.shape[1] // halves
    group_index = lax.axis_index("grp")
    for flip, piece in zip((0,) + ORDER, pieces):
        half = lax.rem(group_index ^ flip, halves)
        for slot in range(slot_count):
            rows = pl.ds(slot * rank + flip // halves * PIECE_ROWS, PIECE_ROWS)
            down[rows, pl.ds(pl.multiple_of(half * wide, 128), wide)] = piece[slot, :, :wide]
            up_ref[rows, pl.ds(pl.multiple_of(half * up_wide, 128), up_wide)] = piece[
                slot, :, wide:
            ]
    rows = shrunk_ref.shape[1]
    slot_of = lax.broadcasted_iota(jnp.int32, shrunk_ref.shape[1:], 1) // rank
    live_count = count_ref[group_index]
    for step in range(x_ref.shape[0]):
        product = lax.dot_general(
            x_ref[step], down[...], (((1,), (1,)), ((), ())), preferred_element_type=jnp.float32
        )
        packed = jnp.zeros(shrunk_ref.shape[1:], jnp.float32)
        for slot in range(slot_count):
            keep = (slot_of == slot) & (slot < live_count)
            packed = jnp.where(keep, product[slot * rows : (slot + 1) * rows], packed)
        shrunk_ref[step] = packed


def expand_kernel(
    slot_count, rank, mine_ref, theirs_ref, up_ref, base_ref, base_other_ref, out_ref, done, sem
):
    rows = mine_ref.shape[1]
    slot_of = lax.broadcasted_iota(jnp.int32, mine_ref.shape[1:], 1) // rank
    up = up_ref[...]
    up_thrice = jnp.concatenate([up, up, up], axis=0)
    for step in range(mine_ref.shape[0]):
        shrunk = mine_ref[step] + theirs_ref[step]
        top = shrunk.astype(jnp.bfloat16)
        rest = shrunk - top.astype(jnp.float32)
        mid = rest.astype(jnp.bfloat16)
        low = (rest - mid.astype(jnp.float32)).astype(jnp.bfloat16)
        zero = jnp.zeros_like(top)
        for slot in range(slot_count):
            terms = jnp.concatenate(
                [jnp.where(slot_of == slot, term, zero) for term in (top, mid, low)], axis=1
            )
            expanded = jnp.dot(terms, up_thrice, preferred_element_type=jnp.float32)
            at = pl.ds((step * slot_count + slot) * rows, rows)
            total = base_ref[at, :] + base_other_ref[at, :]
            done[step, pl.ds(slot * rows, rows), :] = (total + adapter_scale_factor * expanded).astype(done.dtype)
        pltpu.make_async_copy(done.at[step], out_ref.at[step], sem.at[step]).start()
    for step in range(mine_ref.shape[0]):
        pltpu.make_async_copy(done.at[step], out_ref.at[step], sem.at[step]).wait()


def local(hidden, base_weight, pool_down, pool_up, adapter_home, block_adapter, block_count):
    step_count, row_count, half_width = hidden.shape
    rep_count = lax.axis_size("rep")
    group_count = lax.axis_size("grp")
    rank = pool_up.shape[1]
    col_count = pool_up.shape[2]
    slot_count = block_adapter.shape[1]
    block_rows = row_count // slot_count
    share = col_count // lax.axis_size("tp")
    near = MEMBERS // rep_count
    halves = MEMBERS * PIECE_ROWS // rank
    piece_width = (half_width + share) // halves
    bf16, f32 = jnp.bfloat16, jnp.float32

    down = jnp.swapaxes(pool_down[0], 0, 1)
    packed = pl.pallas_call(
        functools.partial(pack_kernel, near, halves),
        out_shape=pltpu.VMEM((group_count, PIECE_ROWS, piece_width), bf16),
        in_specs=[ANY, ANY],
        out_specs=VMEM,
        scratch_shapes=[pltpu.SemaphoreType.DMA((2 * group_count,))],
        compiler_params=pltpu.CompilerParams(vmem_limit_bytes=56 << 20),
        name="pack",
    )(down, pool_up[0])
    held = lax.all_to_all(packed, "grp", 0, 0, tiled=True)
    asked = jnp.swapaxes(block_adapter, 0, 1)
    wanted = [asked]
    for flip in range(1, rep_count):
        pairs = [(r, r ^ flip) for r in range(rep_count)]
        wanted.append(lax.ppermute(asked, "rep", pairs))

    chunk_count = 4
    chunk = half_width // chunk_count
    rows = step_count * row_count
    mine, theirs = pl.pallas_call(
        base_kernel,
        grid=(chunk_count,),
        out_shape=[jax.ShapeDtypeStruct((rows, share), f32)] * 2,
        in_specs=[
            pl.BlockSpec((step_count, row_count, chunk), lambda k: (0, 0, k)),
            pl.BlockSpec((chunk, col_count), lambda k: (k, 0)),
        ],
        out_specs=[pl.BlockSpec((rows, share), lambda k: (0, 0))] * 2,
        compiler_params=pltpu.CompilerParams(vmem_limit_bytes=52 << 20),
        cost_estimate=pl.CostEstimate(
            flops=2 * rows * half_width * col_count,
            bytes_accessed=2 * rows * (half_width + 4 * share),
            transcendentals=0,
        ),
        name="base",
    )(hidden, base_weight)
    swap = [(0, 1), (1, 0)]
    base_other = lax.ppermute(theirs, "tp", swap)
    held, wanted[1:], mine, base_other = lax.optimization_barrier(
        (held, wanted[1:], mine, base_other)
    )

    sends = pl.pallas_call(
        functools.partial(select_kernel, near, rep_count),
        out_shape=[jax.ShapeDtypeStruct((slot_count, PIECE_ROWS, piece_width), bf16)] * MEMBERS,
        in_specs=[SMEM] * (1 + rep_count) + [VMEM],
        out_specs=[VMEM] * MEMBERS,
        compiler_params=pltpu.CompilerParams(vmem_limit_bytes=12 << 20),
        name="select",
    )(adapter_home, *wanted, held)
    got = []
    for flip, send in zip(ORDER, sends[1:]):
        pairs = [
            (r * group_count + g, (r ^ flip // near) * group_count + (g ^ flip % near))
            for r in range(rep_count)
            for g in range(group_count)
        ]
        got.append(lax.ppermute(send, ("rep", "grp"), pairs))

    late, own = lax.optimization_barrier((hidden, sends[0]))
    near_hidden = pl.pallas_call(
        stage_kernel,
        out_shape=pltpu.VMEM(hidden.shape, bf16),
        in_specs=[ANY],
        out_specs=VMEM,
        scratch_shapes=[pltpu.SemaphoreType.DMA(())],
        compiler_params=pltpu.CompilerParams(vmem_limit_bytes=48 << 20),
        cost_estimate=pl.CostEstimate(
            flops=0, bytes_accessed=4 * hidden.size, transcendentals=0
        ),
        name="stage",
    )(late)

    both = slot_count * rank
    shrunk, up = pl.pallas_call(
        functools.partial(shrink_kernel, halves, rank),
        out_shape=[
            jax.ShapeDtypeStruct((step_count, block_rows, both), f32),
            jax.ShapeDtypeStruct((both, share), bf16),
        ],
        in_specs=[SMEM] + [VMEM] * (1 + MEMBERS),
        out_specs=[VMEM, VMEM],
        scratch_shapes=[pltpu.VMEM((both, half_width), bf16)],
        compiler_params=pltpu.CompilerParams(vmem_limit_bytes=12 << 20),
        cost_estimate=pl.CostEstimate(
            flops=2 * rows * half_width * both,
            bytes_accessed=2 * rows * half_width,
            transcendentals=0,
        ),
        name="shrink",
    )(block_count, near_hidden, own, *got)
    shrunk_other = lax.ppermute(shrunk, "tp", swap)

    return pl.pallas_call(
        functools.partial(expand_kernel, slot_count, rank),
        out_shape=jax.ShapeDtypeStruct((step_count, row_count, share), bf16),
        in_specs=[VMEM] * 5,
        out_specs=ANY,
        scratch_shapes=[
            pltpu.VMEM((step_count, row_count, share), bf16),
            pltpu.SemaphoreType.DMA((step_count,)),
        ],
        compiler_params=pltpu.CompilerParams(vmem_limit_bytes=12 << 20),
        name="expand",
    )(shrunk, shrunk_other, up, mine, base_other)


def solution(mesh):
    in_specs = (
        P(None, ("rep", "grp"), "tp"),
        P("tp", None),
        P("grp", "tp", None),
        P("grp", None, None),
        P(),
        P("rep", None),
        P("rep"),
    )
    out_specs = P(None, ("rep", "grp"), "tp")
    return jax.shard_map(local, mesh=mesh, in_specs=in_specs, out_specs=out_specs, check_vma=False)
```

```python
import functools

import jax
import jax.numpy as jnp
from jax import lax
from jax.experimental import pallas as pl
from jax.experimental.pallas import tpu as pltpu
from jax.sharding import PartitionSpec as P

adapter_scale_factor = 0.5
MEMBERS = 8
PIECE_ROWS = 16

ANY = pl.BlockSpec(memory_space=pl.ANY)
SMEM = pl.BlockSpec(memory_space=pltpu.SMEM)
VMEM = pl.BlockSpec(memory_space=pltpu.VMEM)


def pack_kernel(near, halves, down_ref, up_ref, out_ref, down, up, sem):
    tall, up_own = up.shape
    rows = pl.ds(pl.multiple_of(lax.axis_index("rep") * tall, tall), tall)
    columns = pl.ds(pl.multiple_of(lax.axis_index("tp") * up_own, 128), up_own)
    copies = [
        pltpu.make_async_copy(down_ref.at[rows], down, sem.at[0]),
        pltpu.make_async_copy(up_ref.at[rows, columns], up, sem.at[1]),
    ]
    for copy in copies:
        copy.start()
    for copy in copies:
        copy.wait()
    wide, up_wide = down.shape[1] // halves, up_own // halves
    for group in range(out_ref.shape[0]):
        place, half = group % near // halves, group % halves
        rows = slice(place * PIECE_ROWS, (place + 1) * PIECE_ROWS)
        out_ref[group, :, :wide] = down[rows, half * wide : (half + 1) * wide]
        out_ref[group, :, wide:] = up[rows, half * up_wide : (half + 1) * up_wide]


def select_kernel(near, halves, crossing, rep_count, home_ref, *refs):
    wanted, held_ref, (plane_ref, *outs) = refs[:rep_count], refs[rep_count], refs[rep_count + 1 :]
    group_index = lax.axis_index("grp")
    rep_index = lax.axis_index("rep")
    pool_size = home_ref.shape[0]

    def fill(out_ref, flip, other):
        for slot in range(out_ref.shape[0]):
            adapter = jnp.clip(wanted[flip][slot, other], 0, pool_size - 1)
            place = jnp.clip(home_ref[adapter], 0, pool_size - 1)
            out_ref[slot] = held_ref[place]

    for flip, out_ref in zip(crossing, outs):
        fill(out_ref, flip // near, group_index ^ (flip % near))
    for flip in range(rep_count):
        for half in range(halves):
            fill(
                plane_ref.at[(rep_index ^ flip) * halves + half],
                flip,
                group_index // halves * halves + half,
            )


def stage_kernel(x_ref, out_ref, sem):
    copy = pltpu.make_async_copy(x_ref, out_ref, sem)
    copy.start()
    copy.wait()


def base_kernel(x_ref, weight_ref, mine_ref, theirs_ref):
    rows, share = mine_ref.shape
    x = x_ref[...].reshape(rows, x_ref.shape[2])
    product = jnp.dot(x, weight_ref[...], preferred_element_type=jnp.float32)
    first, second = product[:, :share], product[:, share:]
    tp_index = lax.axis_index("tp")
    fresh = pl.program_id(0) == 0

    def store(mine, theirs):
        @pl.when(fresh)
        def _():
            mine_ref[...] = mine
            theirs_ref[...] = theirs

        @pl.when(jnp.logical_not(fresh))
        def _():
            mine_ref[...] += mine
            theirs_ref[...] += theirs

    @pl.when(tp_index == 0)
    def _():
        store(first, second)

    @pl.when(tp_index == 1)
    def _():
        store(second, first)


def shrink_kernel(near, halves, crossing, rank, count_ref, x_ref, plane_ref, *refs):
    pieces, (shrunk_ref, up_ref, down) = refs[:-3], refs[-3:]
    slot_count = plane_ref.shape[1]
    wide = down.shape[1] // halves
    up_wide = up_ref.shape[1] // halves
    group_index = lax.axis_index("grp")
    low = lax.rem(group_index, near)
    me = lax.axis_index("rep") * near + low

    def put(member, half, piece_ref):
        for slot in range(slot_count):
            row = slot * rank + member // halves * PIECE_ROWS
            rows = pl.ds(pl.multiple_of(row, PIECE_ROWS), PIECE_ROWS)
            down[rows, pl.ds(pl.multiple_of(half * wide, 128), wide)] = piece_ref[slot, :, :wide]
            up_ref[rows, pl.ds(pl.multiple_of(half * up_wide, 128), up_wide)] = piece_ref[
                slot, :, wide:
            ]

    for flip, piece_ref in zip(crossing, pieces):
        put(me ^ flip, lax.rem(me ^ flip, halves), piece_ref)
    for at in range(plane_ref.shape[0]):
        put(at // halves * near + low // halves * halves, at % halves, plane_ref.at[at])
    rows = shrunk_ref.shape[1]
    slot_of = lax.broadcasted_iota(jnp.int32, shrunk_ref.shape[1:], 1) // rank
    live_count = count_ref[group_index]
    for step in range(x_ref.shape[0]):
        product = lax.dot_general(
            x_ref[step], down[...], (((1,), (1,)), ((), ())), preferred_element_type=jnp.float32
        )
        packed = jnp.zeros(shrunk_ref.shape[1:], jnp.float32)
        for slot in range(slot_count):
            keep = (slot_of == slot) & (slot < live_count)
            packed = jnp.where(keep, product[slot * rows : (slot + 1) * rows], packed)
        shrunk_ref[step] = packed


def expand_kernel(
    slot_count, rank, mine_ref, theirs_ref, up_ref, base_ref, base_other_ref, out_ref, done, sem
):
    rows = mine_ref.shape[1]
    slot_of = lax.broadcasted_iota(jnp.int32, mine_ref.shape[1:], 1) // rank
    up = up_ref[...]
    up_thrice = jnp.concatenate([up, up, up], axis=0)
    for step in range(mine_ref.shape[0]):
        shrunk = mine_ref[step] + theirs_ref[step]
        top = shrunk.astype(jnp.bfloat16)
        rest = shrunk - top.astype(jnp.float32)
        mid = rest.astype(jnp.bfloat16)
        low = (rest - mid.astype(jnp.float32)).astype(jnp.bfloat16)
        zero = jnp.zeros_like(top)
        for slot in range(slot_count):
            terms = jnp.concatenate(
                [jnp.where(slot_of == slot, term, zero) for term in (top, mid, low)], axis=1
            )
            expanded = jnp.dot(terms, up_thrice, preferred_element_type=jnp.float32)
            at = pl.ds((step * slot_count + slot) * rows, rows)
            total = base_ref[at, :] + base_other_ref[at, :]
            done[step, pl.ds(slot * rows, rows), :] = (total + adapter_scale_factor * expanded).astype(done.dtype)
        pltpu.make_async_copy(done.at[step], out_ref.at[step], sem.at[step]).start()
    for step in range(mine_ref.shape[0]):
        pltpu.make_async_copy(done.at[step], out_ref.at[step], sem.at[step]).wait()


def local(hidden, base_weight, pool_down, pool_up, adapter_home, block_adapter, block_count):
    step_count, row_count, half_width = hidden.shape
    rep_count = lax.axis_size("rep")
    group_count = lax.axis_size("grp")
    rank = pool_up.shape[1]
    col_count = pool_up.shape[2]
    slot_count = block_adapter.shape[1]
    block_rows = row_count // slot_count
    share = col_count // lax.axis_size("tp")
    near = MEMBERS // rep_count
    halves = MEMBERS * PIECE_ROWS // rank
    piece_width = (half_width + share) // halves
    bf16, f32 = jnp.bfloat16, jnp.float32

    down = jnp.swapaxes(pool_down[0], 0, 1)
    packed = pl.pallas_call(
        functools.partial(pack_kernel, near, halves),
        out_shape=pltpu.VMEM((group_count, PIECE_ROWS, piece_width), bf16),
        in_specs=[ANY, ANY],
        out_specs=VMEM,
        scratch_shapes=[
            pltpu.VMEM((rank // rep_count, half_width), bf16),
            pltpu.VMEM((rank // rep_count, share), bf16),
            pltpu.SemaphoreType.DMA((2,)),
        ],
        compiler_params=pltpu.CompilerParams(vmem_limit_bytes=56 << 20),
        name="pack",
    )(down, pool_up[0])
    held = lax.all_to_all(packed, "grp", 0, 0, tiled=True)
    asked = jnp.swapaxes(block_adapter, 0, 1)
    wanted = [asked]
    for flip in range(1, rep_count):
        pairs = [(r, r ^ flip) for r in range(rep_count)]
        wanted.append(lax.ppermute(asked, "rep", pairs))

    chunk_count = 4
    chunk = half_width // chunk_count
    rows = step_count * row_count
    mine, theirs = pl.pallas_call(
        base_kernel,
        grid=(chunk_count,),
        out_shape=[jax.ShapeDtypeStruct((rows, share), f32)] * 2,
        in_specs=[
            pl.BlockSpec((step_count, row_count, chunk), lambda k: (0, 0, k)),
            pl.BlockSpec((chunk, col_count), lambda k: (k, 0)),
        ],
        out_specs=[pl.BlockSpec((rows, share), lambda k: (0, 0))] * 2,
        compiler_params=pltpu.CompilerParams(vmem_limit_bytes=52 << 20),
        cost_estimate=pl.CostEstimate(
            flops=2 * rows * half_width * col_count,
            bytes_accessed=2 * rows * (half_width + 4 * share),
            transcendentals=0,
        ),
        name="base",
    )(hidden, base_weight)
    swap = [(0, 1), (1, 0)]
    base_other = lax.ppermute(theirs, "tp", swap)
    held, wanted[1:], mine, base_other = lax.optimization_barrier(
        (held, wanted[1:], mine, base_other)
    )

    crossing = [flip for flip in range(MEMBERS - 1, 0, -1) if flip % near >= halves]
    plane_size = rep_count * halves
    piece_shape = (slot_count, PIECE_ROWS, piece_width)
    plane, *sends = pl.pallas_call(
        functools.partial(select_kernel, near, halves, crossing, rep_count),
        out_shape=[jax.ShapeDtypeStruct((plane_size, *piece_shape), bf16)]
        + [jax.ShapeDtypeStruct(piece_shape, bf16)] * len(crossing),
        in_specs=[SMEM] * (1 + rep_count) + [VMEM],
        out_specs=[VMEM] * (1 + len(crossing)),
        compiler_params=pltpu.CompilerParams(vmem_limit_bytes=12 << 20),
        name="select",
    )(adapter_home, *wanted, held)
    got = []
    for flip, send in zip(crossing, sends):
        pairs = [
            (r * group_count + g, (r ^ flip // near) * group_count + (g ^ flip % near))
            for r in range(rep_count)
            for g in range(group_count)
        ]
        got.append(lax.ppermute(send, ("rep", "grp"), pairs))
    groups = [
        [r * group_count + g for r in range(rep_count) for g in range(first, first + halves)]
        for first in range(0, group_count, halves)
    ]
    got_plane = lax.all_to_all(
        plane, ("rep", "grp"), 0, 0, axis_index_groups=groups, tiled=True
    )

    late, got_plane = lax.optimization_barrier((hidden, got_plane))
    near_hidden = pl.pallas_call(
        stage_kernel,
        out_shape=pltpu.VMEM(hidden.shape, bf16),
        in_specs=[ANY],
        out_specs=VMEM,
        scratch_shapes=[pltpu.SemaphoreType.DMA(())],
        compiler_params=pltpu.CompilerParams(vmem_limit_bytes=48 << 20),
        cost_estimate=pl.CostEstimate(
            flops=0, bytes_accessed=4 * hidden.size, transcendentals=0
        ),
        name="stage",
    )(late)

    both = slot_count * rank
    shrunk, up = pl.pallas_call(
        functools.partial(shrink_kernel, near, halves, crossing, rank),
        out_shape=[
            jax.ShapeDtypeStruct((step_count, block_rows, both), f32),
            jax.ShapeDtypeStruct((both, share), bf16),
        ],
        in_specs=[SMEM] + [VMEM] * (2 + len(crossing)),
        out_specs=[VMEM, VMEM],
        scratch_shapes=[pltpu.VMEM((both, half_width), bf16)],
        compiler_params=pltpu.CompilerParams(vmem_limit_bytes=12 << 20),
        cost_estimate=pl.CostEstimate(
            flops=2 * rows * half_width * both,
            bytes_accessed=2 * rows * half_width,
            transcendentals=0,
        ),
        name="shrink",
    )(block_count, near_hidden, got_plane, *got)
    shrunk_other = lax.ppermute(shrunk, "tp", swap)

    return pl.pallas_call(
        functools.partial(expand_kernel, slot_count, rank),
        out_shape=jax.ShapeDtypeStruct((step_count, row_count, share), bf16),
        in_specs=[VMEM] * 5,
        out_specs=ANY,
        scratch_shapes=[
            pltpu.VMEM((step_count, row_count, share), bf16),
            pltpu.SemaphoreType.DMA((step_count,)),
        ],
        compiler_params=pltpu.CompilerParams(vmem_limit_bytes=12 << 20),
        name="expand",
    )(shrunk, shrunk_other, up, mine, base_other)


def solution(mesh):
    in_specs = (
        P(None, ("rep", "grp"), "tp"),
        P("tp", None),
        P("grp", "tp", None),
        P("grp", None, None),
        P(),
        P("rep", None),
        P("rep"),
    )
    out_specs = P(None, ("rep", "grp"), "tp")
    return jax.shard_map(local, mesh=mesh, in_specs=in_specs, out_specs=out_specs, check_vma=False)
```

```python
import functools

import jax
import jax.numpy as jnp
from jax import lax
from jax.experimental import pallas as pl
from jax.experimental.pallas import tpu as pltpu
from jax.sharding import PartitionSpec as P

adapter_scale_factor = 0.5
MEMBERS = 8
PIECE_ROWS = 16
ORDER = (4, 2, 1, 7, 6, 5, 3)

ANY = pl.BlockSpec(memory_space=pl.ANY)
SMEM = pl.BlockSpec(memory_space=pltpu.SMEM)
VMEM = pl.BlockSpec(memory_space=pltpu.VMEM)


def pack_kernel(near, halves, down_ref, up_ref, out_ref, down, up, sem):
    tall, up_own = up.shape
    rows = pl.ds(pl.multiple_of(lax.axis_index("rep") * tall, tall), tall)
    columns = pl.ds(pl.multiple_of(lax.axis_index("tp") * up_own, 128), up_own)
    copies = [
        pltpu.make_async_copy(down_ref.at[rows], down, sem.at[0]),
        pltpu.make_async_copy(up_ref.at[rows, columns], up, sem.at[1]),
    ]
    for copy in copies:
        copy.start()
    for copy in copies:
        copy.wait()
    wide, up_wide = down.shape[1] // halves, up_own // halves
    for group in range(out_ref.shape[0]):
        place, half = group % near // halves, group % halves
        rows = slice(place * PIECE_ROWS, (place + 1) * PIECE_ROWS)
        out_ref[group, :, :wide] = down[rows, half * wide : (half + 1) * wide]
        out_ref[group, :, wide:] = up[rows, half * up_wide : (half + 1) * up_wide]


def select_kernel(near, rep_count, home_ref, *refs):
    wanted, held_ref, outs = refs[:rep_count], refs[rep_count], refs[rep_count + 1 :]
    group_index = lax.axis_index("grp")
    pool_size = home_ref.shape[0]
    for flip, out in zip((0,) + ORDER, outs):
        other = group_index ^ (flip % near)
        for slot in range(out.shape[0]):
            adapter = jnp.clip(wanted[flip // near][slot, other], 0, pool_size - 1)
            place = jnp.clip(home_ref[adapter], 0, pool_size - 1)
            out[slot] = held_ref[place]


def stage_kernel(x_ref, out_ref, sem):
    copy = pltpu.make_async_copy(x_ref, out_ref, sem)
    copy.start()
    copy.wait()


def base_kernel(x_ref, weight_ref, mine_ref, theirs_ref):
    rows, share = mine_ref.shape
    x = x_ref[...].reshape(rows, x_ref.shape[2])
    product = jnp.dot(x, weight_ref[...], preferred_element_type=jnp.float32)
    first, second = product[:, :share], product[:, share:]
    tp_index = lax.axis_index("tp")
    fresh = pl.program_id(0) == 0

    def store(mine, theirs):
        @pl.when(fresh)
        def _():
            mine_ref[...] = mine
            theirs_ref[...] = theirs

        @pl.when(jnp.logical_not(fresh))
        def _():
            mine_ref[...] += mine
            theirs_ref[...] += theirs

    @pl.when(tp_index == 0)
    def _():
        store(first, second)

    @pl.when(tp_index == 1)
    def _():
        store(second, first)


def shrink_kernel(halves, rank, count_ref, x_ref, *refs):
    pieces, (shrunk_ref, up_ref, down) = refs[:-3], refs[-3:]
    slot_count = pieces[0].shape[0]
    wide = down.shape[1] // halves
    up_wide = up_ref.shape[1] // halves
    group_index = lax.axis_index("grp")
    for flip, piece in zip((0,) + ORDER, pieces):
        half = lax.rem(group_index ^ flip, halves)
        for slot in range(slot_count):
            rows = pl.ds(slot * rank + flip // halves * PIECE_ROWS, PIECE_ROWS)
            down[rows, pl.ds(pl.multiple_of(half * wide, 128), wide)] = piece[slot, :, :wide]
            up_ref[rows, pl.ds(pl.multiple_of(half * up_wide, 128), up_wide)] = piece[
                slot, :, wide:
            ]
    rows = shrunk_ref.shape[1]
    slot_of = lax.broadcasted_iota(jnp.int32, shrunk_ref.shape[1:], 1) // rank
    live_count = count_ref[group_index]
    for step in range(x_ref.shape[0]):
        product = lax.dot_general(
            x_ref[step], down[...], (((1,), (1,)), ((), ())), preferred_element_type=jnp.float32
        )
        packed = jnp.zeros(shrunk_ref.shape[1:], jnp.float32)
        for slot in range(slot_count):
            keep = (slot_of == slot) & (slot < live_count)
            packed = jnp.where(keep, product[slot * rows : (slot + 1) * rows], packed)
        shrunk_ref[step] = packed


def expand_kernel(
    slot_count, rank, mine_ref, theirs_ref, up_ref, base_ref, base_other_ref, out_ref, done, sem
):
    rows = mine_ref.shape[1]
    slot_of = lax.broadcasted_iota(jnp.int32, mine_ref.shape[1:], 1) // rank
    up = up_ref[...]
    up_thrice = jnp.concatenate([up, up, up], axis=0)
    for step in range(mine_ref.shape[0]):
        shrunk = mine_ref[step] + theirs_ref[step]
        top = shrunk.astype(jnp.bfloat16)
        rest = shrunk - top.astype(jnp.float32)
        mid = rest.astype(jnp.bfloat16)
        low = (rest - mid.astype(jnp.float32)).astype(jnp.bfloat16)
        zero = jnp.zeros_like(top)
        for slot in range(slot_count):
            terms = jnp.concatenate(
                [jnp.where(slot_of == slot, term, zero) for term in (top, mid, low)], axis=1
            )
            expanded = jnp.dot(terms, up_thrice, preferred_element_type=jnp.float32)
            at = pl.ds((step * slot_count + slot) * rows, rows)
            total = base_ref[at, :] + base_other_ref[at, :]
            done[step, pl.ds(slot * rows, rows), :] = (total + adapter_scale_factor * expanded).astype(done.dtype)
        pltpu.make_async_copy(done.at[step], out_ref.at[step], sem.at[step]).start()
    for step in range(mine_ref.shape[0]):
        pltpu.make_async_copy(done.at[step], out_ref.at[step], sem.at[step]).wait()


def local(hidden, base_weight, pool_down, pool_up, adapter_home, block_adapter, block_count):
    step_count, row_count, half_width = hidden.shape
    rep_count = lax.axis_size("rep")
    group_count = lax.axis_size("grp")
    rank = pool_up.shape[1]
    col_count = pool_up.shape[2]
    slot_count = block_adapter.shape[1]
    block_rows = row_count // slot_count
    share = col_count // lax.axis_size("tp")
    near = MEMBERS // rep_count
    halves = MEMBERS * PIECE_ROWS // rank
    piece_width = (half_width + share) // halves
    bf16, f32 = jnp.bfloat16, jnp.float32

    down = jnp.swapaxes(pool_down[0], 0, 1)
    packed = pl.pallas_call(
        functools.partial(pack_kernel, near, halves),
        out_shape=pltpu.VMEM((group_count, PIECE_ROWS, piece_width), bf16),
        in_specs=[ANY, ANY],
        out_specs=VMEM,
        scratch_shapes=[
            pltpu.VMEM((rank // rep_count, half_width), bf16),
            pltpu.VMEM((rank // rep_count, share), bf16),
            pltpu.SemaphoreType.DMA((2,)),
        ],
        compiler_params=pltpu.CompilerParams(vmem_limit_bytes=56 << 20),
        name="pack",
    )(down, pool_up[0])
    held = lax.all_to_all(packed, "grp", 0, 0, tiled=True)
    asked = jnp.swapaxes(block_adapter, 0, 1)
    wanted = [asked]
    for flip in range(1, rep_count):
        pairs = [(r, r ^ flip) for r in range(rep_count)]
        wanted.append(lax.ppermute(asked, "rep", pairs))

    chunk_count = 4
    chunk = half_width // chunk_count
    rows = step_count * row_count
    mine, theirs = pl.pallas_call(
        base_kernel,
        grid=(chunk_count,),
        out_shape=[jax.ShapeDtypeStruct((rows, share), f32)] * 2,
        in_specs=[
            pl.BlockSpec((step_count, row_count, chunk), lambda k: (0, 0, k)),
            pl.BlockSpec((chunk, col_count), lambda k: (k, 0)),
        ],
        out_specs=[pl.BlockSpec((rows, share), lambda k: (0, 0))] * 2,
        compiler_params=pltpu.CompilerParams(vmem_limit_bytes=52 << 20),
        cost_estimate=pl.CostEstimate(
            flops=2 * rows * half_width * col_count,
            bytes_accessed=2 * rows * (half_width + 4 * share),
            transcendentals=0,
        ),
        name="base",
    )(hidden, base_weight)
    swap = [(0, 1), (1, 0)]
    base_other = lax.ppermute(theirs, "tp", swap)
    held, wanted[1:], mine, base_other = lax.optimization_barrier(
        (held, wanted[1:], mine, base_other)
    )

    sends = pl.pallas_call(
        functools.partial(select_kernel, near, rep_count),
        out_shape=[jax.ShapeDtypeStruct((slot_count, PIECE_ROWS, piece_width), bf16)] * MEMBERS,
        in_specs=[SMEM] * (1 + rep_count) + [VMEM],
        out_specs=[VMEM] * MEMBERS,
        compiler_params=pltpu.CompilerParams(vmem_limit_bytes=12 << 20),
        name="select",
    )(adapter_home, *wanted, held)
    got = []
    for flip, send in zip(ORDER, sends[1:]):
        pairs = [
            (r * group_count + g, (r ^ flip // near) * group_count + (g ^ flip % near))
            for r in range(rep_count)
            for g in range(group_count)
        ]
        got.append(lax.ppermute(send, ("rep", "grp"), pairs))

    late, own = lax.optimization_barrier((hidden, sends[0]))
    near_hidden = pl.pallas_call(
        stage_kernel,
        out_shape=pltpu.VMEM(hidden.shape, bf16),
        in_specs=[ANY],
        out_specs=VMEM,
        scratch_shapes=[pltpu.SemaphoreType.DMA(())],
        compiler_params=pltpu.CompilerParams(vmem_limit_bytes=48 << 20),
        cost_estimate=pl.CostEstimate(
            flops=0, bytes_accessed=4 * hidden.size, transcendentals=0
        ),
        name="stage",
    )(late)

    both = slot_count * rank
    shrunk, up = pl.pallas_call(
        functools.partial(shrink_kernel, halves, rank),
        out_shape=[
            jax.ShapeDtypeStruct((step_count, block_rows, both), f32),
            jax.ShapeDtypeStruct((both, share), bf16),
        ],
        in_specs=[SMEM] + [VMEM] * (1 + MEMBERS),
        out_specs=[VMEM, VMEM],
        scratch_shapes=[pltpu.VMEM((both, half_width), bf16)],
        compiler_params=pltpu.CompilerParams(vmem_limit_bytes=12 << 20),
        cost_estimate=pl.CostEstimate(
            flops=2 * rows * half_width * both,
            bytes_accessed=2 * rows * half_width,
            transcendentals=0,
        ),
        name="shrink",
    )(block_count, near_hidden, own, *got)
    shrunk_other = lax.ppermute(shrunk, "tp", swap)

    return pl.pallas_call(
        functools.partial(expand_kernel, slot_count, rank),
        out_shape=jax.ShapeDtypeStruct((step_count, row_count, share), bf16),
        in_specs=[VMEM] * 5,
        out_specs=ANY,
        scratch_shapes=[
            pltpu.VMEM((step_count, row_count, share), bf16),
            pltpu.SemaphoreType.DMA((step_count,)),
        ],
        compiler_params=pltpu.CompilerParams(vmem_limit_bytes=12 << 20),
        name="expand",
    )(shrunk, shrunk_other, up, mine, base_other)


def solution(mesh):
    in_specs = (
        P(None, ("rep", "grp"), "tp"),
        P("tp", None),
        P("grp", "tp", None),
        P("grp", None, None),
        P(),
        P("rep", None),
        P("rep"),
    )
    out_specs = P(None, ("rep", "grp"), "tp")
    return jax.shard_map(local, mesh=mesh, in_specs=in_specs, out_specs=out_specs, check_vma=False)
```

```python
import functools

import jax
import jax.numpy as jnp
from jax import lax
from jax.experimental import pallas as pl
from jax.experimental.pallas import tpu as pltpu
from jax.sharding import PartitionSpec as P

adapter_scale_factor = 0.5
MEMBERS = 8
PIECE_ROWS = 16
ORDER = (4, 2, 1, 3, 6, 5, 7)

ANY = pl.BlockSpec(memory_space=pl.ANY)
SMEM = pl.BlockSpec(memory_space=pltpu.SMEM)
VMEM = pl.BlockSpec(memory_space=pltpu.VMEM)


def pack_kernel(near, halves, down_ref, up_ref, out_ref, down, up, sem):
    tall, up_own = up.shape
    rows = pl.ds(pl.multiple_of(lax.axis_index("rep") * tall, tall), tall)
    columns = pl.ds(pl.multiple_of(lax.axis_index("tp") * up_own, 128), up_own)
    copies = [
        pltpu.make_async_copy(down_ref.at[rows], down, sem.at[0]),
        pltpu.make_async_copy(up_ref.at[rows, columns], up, sem.at[1]),
    ]
    for copy in copies:
        copy.start()
    for copy in copies:
        copy.wait()
    wide, up_wide = down.shape[1] // halves, up_own // halves
    for group in range(out_ref.shape[0]):
        place, half = group % near // halves, group % halves
        rows = slice(place * PIECE_ROWS, (place + 1) * PIECE_ROWS)
        out_ref[group, :, :wide] = down[rows, half * wide : (half + 1) * wide]
        out_ref[group, :, wide:] = up[rows, half * up_wide : (half + 1) * up_wide]


def select_kernel(near, rep_count, home_ref, *refs):
    wanted, held_ref, outs = refs[:rep_count], refs[rep_count], refs[rep_count + 1 :]
    group_index = lax.axis_index("grp")
    pool_size = home_ref.shape[0]
    for flip, out in zip((0,) + ORDER, outs):
        other = group_index ^ (flip % near)
        for slot in range(out.shape[0]):
            adapter = jnp.clip(wanted[flip // near][slot, other], 0, pool_size - 1)
            place = jnp.clip(home_ref[adapter], 0, pool_size - 1)
            out[slot] = held_ref[place]


def stage_kernel(x_ref, out_ref, sem):
    copy = pltpu.make_async_copy(x_ref, out_ref, sem)
    copy.start()
    copy.wait()


def base_kernel(x_ref, weight_ref, mine_ref, theirs_ref):
    rows, share = mine_ref.shape
    x = x_ref[...].reshape(rows, x_ref.shape[2])
    product = jnp.dot(x, weight_ref[...], preferred_element_type=jnp.float32)
    first, second = product[:, :share], product[:, share:]
    tp_index = lax.axis_index("tp")
    fresh = pl.program_id(0) == 0

    def store(mine, theirs):
        @pl.when(fresh)
        def _():
            mine_ref[...] = mine
            theirs_ref[...] = theirs

        @pl.when(jnp.logical_not(fresh))
        def _():
            mine_ref[...] += mine
            theirs_ref[...] += theirs

    @pl.when(tp_index == 0)
    def _():
        store(first, second)

    @pl.when(tp_index == 1)
    def _():
        store(second, first)


def shrink_kernel(halves, rank, flips, count_ref, x_ref, *refs):
    pieces, refs = refs[: len(flips)], refs[len(flips) :]
    slot_count = pieces[0].shape[0]
    group_index = lax.axis_index("grp")
    half = lax.rem(group_index ^ flips[0], halves)
    if len(refs) == 3:
        shrunk_ref, up_ref, down = refs
        sum_ref = None
    else:
        sum_ref, part_ref, shrunk_ref, up_ref, down = refs
    wide = down.shape[1]
    up_wide = up_ref.shape[1] if sum_ref is None else part_ref.shape[1]
    if sum_ref is None:
        up_at = slice(None)
    else:
        up_at = pl.ds(pl.multiple_of(half * up_wide, 128), up_wide)
        up_ref[:, pl.ds(pl.multiple_of((1 - half) * up_wide, 128), up_wide)] = part_ref[...]
    for flip, piece in zip(flips, pieces):
        for slot in range(slot_count):
            rows = pl.ds(slot * rank + flip // halves * PIECE_ROWS, PIECE_ROWS)
            down[rows, :] = piece[slot, :, :wide]
            up_ref[rows, up_at] = piece[slot, :, wide:]
    columns = pl.ds(pl.multiple_of(half * wide, 128), wide)
    rows = shrunk_ref.shape[1]
    slot_of = lax.broadcasted_iota(jnp.int32, shrunk_ref.shape[1:], 1) // rank
    live_count = count_ref[group_index]
    for step in range(x_ref.shape[0]):
        product = lax.dot_general(
            x_ref[step, :, columns],
            down[...],
            (((1,), (1,)), ((), ())),
            preferred_element_type=jnp.float32,
        )
        packed = jnp.zeros(shrunk_ref.shape[1:], jnp.float32)
        for slot in range(slot_count):
            keep = (slot_of == slot) & (slot < live_count)
            packed = jnp.where(keep, product[slot * rows : (slot + 1) * rows], packed)
        shrunk_ref[step] = packed if sum_ref is None else packed + sum_ref[step]


def expand_kernel(
    slot_count, rank, mine_ref, theirs_ref, up_ref, base_ref, base_other_ref, out_ref, done, sem
):
    rows = mine_ref.shape[1]
    slot_of = lax.broadcasted_iota(jnp.int32, mine_ref.shape[1:], 1) // rank
    up = up_ref[...]
    up_thrice = jnp.concatenate([up, up, up], axis=0)
    for step in range(mine_ref.shape[0]):
        shrunk = mine_ref[step] + theirs_ref[step]
        top = shrunk.astype(jnp.bfloat16)
        rest = shrunk - top.astype(jnp.float32)
        mid = rest.astype(jnp.bfloat16)
        low = (rest - mid.astype(jnp.float32)).astype(jnp.bfloat16)
        zero = jnp.zeros_like(top)
        for slot in range(slot_count):
            terms = jnp.concatenate(
                [jnp.where(slot_of == slot, term, zero) for term in (top, mid, low)], axis=1
            )
            expanded = jnp.dot(terms, up_thrice, preferred_element_type=jnp.float32)
            at = pl.ds((step * slot_count + slot) * rows, rows)
            total = base_ref[at, :] + base_other_ref[at, :]
            done[step, pl.ds(slot * rows, rows), :] = (total + adapter_scale_factor * expanded).astype(done.dtype)
        pltpu.make_async_copy(done.at[step], out_ref.at[step], sem.at[step]).start()
    for step in range(mine_ref.shape[0]):
        pltpu.make_async_copy(done.at[step], out_ref.at[step], sem.at[step]).wait()


def local(hidden, base_weight, pool_down, pool_up, adapter_home, block_adapter, block_count):
    step_count, row_count, half_width = hidden.shape
    rep_count = lax.axis_size("rep")
    group_count = lax.axis_size("grp")
    rank = pool_up.shape[1]
    col_count = pool_up.shape[2]
    slot_count = block_adapter.shape[1]
    block_rows = row_count // slot_count
    share = col_count // lax.axis_size("tp")
    near = MEMBERS // rep_count
    halves = MEMBERS * PIECE_ROWS // rank
    piece_width = (half_width + share) // halves
    bf16, f32 = jnp.bfloat16, jnp.float32

    down = jnp.swapaxes(pool_down[0], 0, 1)
    packed = pl.pallas_call(
        functools.partial(pack_kernel, near, halves),
        out_shape=pltpu.VMEM((group_count, PIECE_ROWS, piece_width), bf16),
        in_specs=[ANY, ANY],
        out_specs=VMEM,
        scratch_shapes=[
            pltpu.VMEM((rank // rep_count, half_width), bf16),
            pltpu.VMEM((rank // rep_count, share), bf16),
            pltpu.SemaphoreType.DMA((2,)),
        ],
        compiler_params=pltpu.CompilerParams(vmem_limit_bytes=56 << 20),
        name="pack",
    )(down, pool_up[0])
    held = lax.all_to_all(packed, "grp", 0, 0, tiled=True)
    asked = jnp.swapaxes(block_adapter, 0, 1)
    wanted = [asked]
    for flip in range(1, rep_count):
        pairs = [(r, r ^ flip) for r in range(rep_count)]
        wanted.append(lax.ppermute(asked, "rep", pairs))

    chunk_count = 4
    chunk = half_width // chunk_count
    rows = step_count * row_count
    mine, theirs = pl.pallas_call(
        base_kernel,
        grid=(chunk_count,),
        out_shape=[jax.ShapeDtypeStruct((rows, share), f32)] * 2,
        in_specs=[
            pl.BlockSpec((step_count, row_count, chunk), lambda k: (0, 0, k)),
            pl.BlockSpec((chunk, col_count), lambda k: (k, 0)),
        ],
        out_specs=[pl.BlockSpec((rows, share), lambda k: (0, 0))] * 2,
        compiler_params=pltpu.CompilerParams(vmem_limit_bytes=52 << 20),
        cost_estimate=pl.CostEstimate(
            flops=2 * rows * half_width * col_count,
            bytes_accessed=2 * rows * (half_width + 4 * share),
            transcendentals=0,
        ),
        name="base",
    )(hidden, base_weight)
    swap = [(0, 1), (1, 0)]
    base_other = lax.ppermute(theirs, "tp", swap)
    held, wanted[1:], mine, base_other = lax.optimization_barrier(
        (held, wanted[1:], mine, base_other)
    )

    sends = pl.pallas_call(
        functools.partial(select_kernel, near, rep_count),
        out_shape=[jax.ShapeDtypeStruct((slot_count, PIECE_ROWS, piece_width), bf16)] * MEMBERS,
        in_specs=[SMEM] * (1 + rep_count) + [VMEM],
        out_specs=[VMEM] * MEMBERS,
        compiler_params=pltpu.CompilerParams(vmem_limit_bytes=12 << 20),
        name="select",
    )(adapter_home, *wanted, held)
    got = []
    for flip, send in zip(ORDER, sends[1:]):
        pairs = [
            (r * group_count + g, (r ^ flip // near) * group_count + (g ^ flip % near))
            for r in range(rep_count)
            for g in range(group_count)
        ]
        got.append(lax.ppermute(send, ("rep", "grp"), pairs))

    late, own = lax.optimization_barrier((hidden, sends[0]))
    near_hidden = pl.pallas_call(
        stage_kernel,
        out_shape=pltpu.VMEM(hidden.shape, bf16),
        in_specs=[ANY],
        out_specs=VMEM,
        scratch_shapes=[pltpu.SemaphoreType.DMA(())],
        compiler_params=pltpu.CompilerParams(vmem_limit_bytes=48 << 20),
        cost_estimate=pl.CostEstimate(
            flops=0, bytes_accessed=4 * hidden.size, transcendentals=0
        ),
        name="stage",
    )(late)

    both = slot_count * rank
    got[:5] = lax.optimization_barrier(tuple(got[:5]))
    arrived = [own, *got]
    parts = ()
    for change in range(halves):
        mine_at = [at for at, flip in enumerate((0,) + ORDER) if flip % halves == change]
        up_width = share if change else share // halves
        parts = pl.pallas_call(
            functools.partial(
                shrink_kernel, halves, rank, [((0,) + ORDER)[at] for at in mine_at]
            ),
            out_shape=[
                jax.ShapeDtypeStruct((step_count, block_rows, both), f32),
                jax.ShapeDtypeStruct((both, up_width), bf16),
            ],
            in_specs=[SMEM] + [VMEM] * (1 + len(mine_at) + len(parts)),
            out_specs=[VMEM, VMEM],
            scratch_shapes=[pltpu.VMEM((both, half_width // halves), bf16)],
            compiler_params=pltpu.CompilerParams(vmem_limit_bytes=12 << 20),
            cost_estimate=pl.CostEstimate(
                flops=2 * rows * half_width * both // halves,
                bytes_accessed=2 * rows * half_width // halves,
                transcendentals=0,
            ),
            name="shrink",
        )(block_count, near_hidden, *(arrived[at] for at in mine_at), *parts)
    shrunk, up = parts
    shrunk_other = lax.ppermute(shrunk, "tp", swap)

    return pl.pallas_call(
        functools.partial(expand_kernel, slot_count, rank),
        out_shape=jax.ShapeDtypeStruct((step_count, row_count, share), bf16),
        in_specs=[VMEM] * 5,
        out_specs=ANY,
        scratch_shapes=[
            pltpu.VMEM((step_count, row_count, share), bf16),
            pltpu.SemaphoreType.DMA((step_count,)),
        ],
        compiler_params=pltpu.CompilerParams(vmem_limit_bytes=12 << 20),
        name="expand",
    )(shrunk, shrunk_other, up, mine, base_other)


def solution(mesh):
    in_specs = (
        P(None, ("rep", "grp"), "tp"),
        P("tp", None),
        P("grp", "tp", None),
        P("grp", None, None),
        P(),
        P("rep", None),
        P("rep"),
    )
    out_specs = P(None, ("rep", "grp"), "tp")
    return jax.shard_map(local, mesh=mesh, in_specs=in_specs, out_specs=out_specs, check_vma=False)
```

```python
import functools

import jax
import jax.numpy as jnp
from jax import lax
from jax.experimental import pallas as pl
from jax.experimental.pallas import tpu as pltpu
from jax.sharding import PartitionSpec as P

adapter_scale_factor = 0.5
MEMBERS = 8
PIECE_ROWS = 16
ORDER = (4, 2, 1, 3, 6, 5, 7)

ANY = pl.BlockSpec(memory_space=pl.ANY)
SMEM = pl.BlockSpec(memory_space=pltpu.SMEM)
VMEM = pl.BlockSpec(memory_space=pltpu.VMEM)


def pack_kernel(near, halves, down_ref, up_ref, out_ref, down, up, sem):
    tall, up_own = up.shape
    rows = pl.ds(pl.multiple_of(lax.axis_index("rep") * tall, tall), tall)
    columns = pl.ds(pl.multiple_of(lax.axis_index("tp") * up_own, 128), up_own)
    copies = [
        pltpu.make_async_copy(down_ref.at[rows], down, sem.at[0]),
        pltpu.make_async_copy(up_ref.at[rows, columns], up, sem.at[1]),
    ]
    for copy in copies:
        copy.start()
    for copy in copies:
        copy.wait()
    wide, up_wide = down.shape[1] // halves, up_own // halves
    for group in range(out_ref.shape[0]):
        place, half = group % near // halves, group % halves
        rows = slice(place * PIECE_ROWS, (place + 1) * PIECE_ROWS)
        out_ref[group, :, :wide] = down[rows, half * wide : (half + 1) * wide]
        out_ref[group, :, wide:] = up[rows, half * up_wide : (half + 1) * up_wide]


def select_kernel(near, rep_count, home_ref, *refs):
    wanted, held_ref, outs = refs[:rep_count], refs[rep_count], refs[rep_count + 1 :]
    group_index = lax.axis_index("grp")
    pool_size = home_ref.shape[0]
    for flip, out in zip((0,) + ORDER, outs):
        other = group_index ^ (flip % near)
        for slot in range(out.shape[0]):
            adapter = jnp.clip(wanted[flip // near][slot, other], 0, pool_size - 1)
            place = jnp.clip(home_ref[adapter], 0, pool_size - 1)
            out[slot] = held_ref[place]


def stage_kernel(x_ref, out_ref, sem):
    copy = pltpu.make_async_copy(x_ref, out_ref, sem)
    copy.start()
    copy.wait()


def base_kernel(x_ref, weight_ref, mine_ref, theirs_ref):
    rows, share = mine_ref.shape
    x = x_ref[...].reshape(rows, x_ref.shape[2])
    product = jnp.dot(x, weight_ref[...], preferred_element_type=jnp.float32)
    first, second = product[:, :share], product[:, share:]
    tp_index = lax.axis_index("tp")
    fresh = pl.program_id(0) == 0

    def store(mine, theirs):
        @pl.when(fresh)
        def _():
            mine_ref[...] = mine
            theirs_ref[...] = theirs

        @pl.when(jnp.logical_not(fresh))
        def _():
            mine_ref[...] += mine
            theirs_ref[...] += theirs

    @pl.when(tp_index == 0)
    def _():
        store(first, second)

    @pl.when(tp_index == 1)
    def _():
        store(second, first)


def shrink_kernel(halves, rank, flips, count_ref, x_ref, *refs):
    pieces, refs = refs[: len(flips)], refs[len(flips) :]
    slot_count = pieces[0].shape[0]
    group_index = lax.axis_index("grp")
    half = lax.rem(group_index ^ flips[0], halves)
    if len(refs) == 3:
        shrunk_ref, up_ref, down = refs
        sum_ref = None
    else:
        sum_ref, part_ref, shrunk_ref, up_ref, down = refs
    wide = down.shape[1]
    up_wide = up_ref.shape[1] if sum_ref is None else part_ref.shape[1]
    if sum_ref is None:
        up_at = slice(None)
    else:
        up_at = pl.ds(pl.multiple_of(half * up_wide, 128), up_wide)
        up_ref[:, pl.ds(pl.multiple_of((1 - half) * up_wide, 128), up_wide)] = part_ref[...]
    for flip, piece in zip(flips, pieces):
        for slot in range(slot_count):
            rows = pl.ds(slot * rank + flip // halves * PIECE_ROWS, PIECE_ROWS)
            down[rows, :] = piece[slot, :, :wide]
            up_ref[rows, up_at] = piece[slot, :, wide:]
    columns = pl.ds(pl.multiple_of(half * wide, 128), wide)
    rows = shrunk_ref.shape[1]
    slot_of = lax.broadcasted_iota(jnp.int32, shrunk_ref.shape[1:], 1) // rank
    live_count = count_ref[group_index]
    for step in range(x_ref.shape[0]):
        product = lax.dot_general(
            x_ref[step, :, columns],
            down[...],
            (((1,), (1,)), ((), ())),
            preferred_element_type=jnp.float32,
        )
        packed = jnp.zeros(shrunk_ref.shape[1:], jnp.float32)
        for slot in range(slot_count):
            keep = (slot_of == slot) & (slot < live_count)
            packed = jnp.where(keep, product[slot * rows : (slot + 1) * rows], packed)
        shrunk_ref[step] = packed if sum_ref is None else packed + sum_ref[step]


def expand_kernel(
    slot_count, rank, mine_ref, theirs_ref, up_ref, base_ref, base_other_ref, out_ref, done, sem
):
    rows = mine_ref.shape[1]
    slot_of = lax.broadcasted_iota(jnp.int32, mine_ref.shape[1:], 1) // rank
    up = up_ref[...]
    up_thrice = jnp.concatenate([up, up, up], axis=0)
    terms = []
    for step in range(mine_ref.shape[0]):
        shrunk = mine_ref[step] + theirs_ref[step]
        top = shrunk.astype(jnp.bfloat16)
        rest = shrunk - top.astype(jnp.float32)
        mid = rest.astype(jnp.bfloat16)
        low = (rest - mid.astype(jnp.float32)).astype(jnp.bfloat16)
        zero = jnp.zeros_like(top)
        for slot in range(slot_count):
            terms.append(
                jnp.concatenate(
                    [jnp.where(slot_of == slot, term, zero) for term in (top, mid, low)], axis=1
                )
            )
    products = jnp.dot(
        jnp.concatenate(terms, axis=0), up_thrice, preferred_element_type=jnp.float32
    )
    tall = slot_count * rows
    for step in range(mine_ref.shape[0]):
        at = slice(step * tall, (step + 1) * tall)
        total = base_ref[at, :] + base_other_ref[at, :]
        done[step] = (total + adapter_scale_factor * products[at]).astype(done.dtype)
        pltpu.make_async_copy(done.at[step], out_ref.at[step], sem.at[step]).start()
    for step in range(mine_ref.shape[0]):
        pltpu.make_async_copy(done.at[step], out_ref.at[step], sem.at[step]).wait()


def local(hidden, base_weight, pool_down, pool_up, adapter_home, block_adapter, block_count):
    step_count, row_count, half_width = hidden.shape
    rep_count = lax.axis_size("rep")
    group_count = lax.axis_size("grp")
    rank = pool_up.shape[1]
    col_count = pool_up.shape[2]
    slot_count = block_adapter.shape[1]
    block_rows = row_count // slot_count
    share = col_count // lax.axis_size("tp")
    near = MEMBERS // rep_count
    halves = MEMBERS * PIECE_ROWS // rank
    piece_width = (half_width + share) // halves
    bf16, f32 = jnp.bfloat16, jnp.float32

    down = jnp.swapaxes(pool_down[0], 0, 1)
    packed = pl.pallas_call(
        functools.partial(pack_kernel, near, halves),
        out_shape=pltpu.VMEM((group_count, PIECE_ROWS, piece_width), bf16),
        in_specs=[ANY, ANY],
        out_specs=VMEM,
        scratch_shapes=[
            pltpu.VMEM((rank // rep_count, half_width), bf16),
            pltpu.VMEM((rank // rep_count, share), bf16),
            pltpu.SemaphoreType.DMA((2,)),
        ],
        compiler_params=pltpu.CompilerParams(vmem_limit_bytes=56 << 20),
        name="pack",
    )(down, pool_up[0])
    held = lax.all_to_all(packed, "grp", 0, 0, tiled=True)
    asked = jnp.swapaxes(block_adapter, 0, 1)
    wanted = [asked]
    for flip in range(1, rep_count):
        pairs = [(r, r ^ flip) for r in range(rep_count)]
        wanted.append(lax.ppermute(asked, "rep", pairs))

    chunk_count = 4
    chunk = half_width // chunk_count
    rows = step_count * row_count
    mine, theirs = pl.pallas_call(
        base_kernel,
        grid=(chunk_count,),
        out_shape=[jax.ShapeDtypeStruct((rows, share), f32)] * 2,
        in_specs=[
            pl.BlockSpec((step_count, row_count, chunk), lambda k: (0, 0, k)),
            pl.BlockSpec((chunk, col_count), lambda k: (k, 0)),
        ],
        out_specs=[pl.BlockSpec((rows, share), lambda k: (0, 0))] * 2,
        compiler_params=pltpu.CompilerParams(vmem_limit_bytes=52 << 20),
        cost_estimate=pl.CostEstimate(
            flops=2 * rows * half_width * col_count,
            bytes_accessed=2 * rows * (half_width + 4 * share),
            transcendentals=0,
        ),
        name="base",
    )(hidden, base_weight)
    swap = [(0, 1), (1, 0)]
    base_other = lax.ppermute(theirs, "tp", swap)
    held, wanted[1:], mine, base_other = lax.optimization_barrier(
        (held, wanted[1:], mine, base_other)
    )

    sends = pl.pallas_call(
        functools.partial(select_kernel, near, rep_count),
        out_shape=[jax.ShapeDtypeStruct((slot_count, PIECE_ROWS, piece_width), bf16)] * MEMBERS,
        in_specs=[SMEM] * (1 + rep_count) + [VMEM],
        out_specs=[VMEM] * MEMBERS,
        compiler_params=pltpu.CompilerParams(vmem_limit_bytes=12 << 20),
        name="select",
    )(adapter_home, *wanted, held)
    got = []
    for flip, send in zip(ORDER, sends[1:]):
        pairs = [
            (r * group_count + g, (r ^ flip // near) * group_count + (g ^ flip % near))
            for r in range(rep_count)
            for g in range(group_count)
        ]
        got.append(lax.ppermute(send, ("rep", "grp"), pairs))

    late, own = lax.optimization_barrier((hidden, sends[0]))
    near_hidden = pl.pallas_call(
        stage_kernel,
        out_shape=pltpu.VMEM(hidden.shape, bf16),
        in_specs=[ANY],
        out_specs=VMEM,
        scratch_shapes=[pltpu.SemaphoreType.DMA(())],
        compiler_params=pltpu.CompilerParams(vmem_limit_bytes=48 << 20),
        cost_estimate=pl.CostEstimate(
            flops=0, bytes_accessed=4 * hidden.size, transcendentals=0
        ),
        name="stage",
    )(late)

    both = slot_count * rank
    got[:5] = lax.optimization_barrier(tuple(got[:5]))
    arrived = [own, *got]
    parts = ()
    for change in range(halves):
        mine_at = [at for at, flip in enumerate((0,) + ORDER) if flip % halves == change]
        up_width = share if change else share // halves
        parts = pl.pallas_call(
            functools.partial(
                shrink_kernel, halves, rank, [((0,) + ORDER)[at] for at in mine_at]
            ),
            out_shape=[
                jax.ShapeDtypeStruct((step_count, block_rows, both), f32),
                jax.ShapeDtypeStruct((both, up_width), bf16),
            ],
            in_specs=[SMEM] + [VMEM] * (1 + len(mine_at) + len(parts)),
            out_specs=[VMEM, VMEM],
            scratch_shapes=[pltpu.VMEM((both, half_width // halves), bf16)],
            compiler_params=pltpu.CompilerParams(vmem_limit_bytes=12 << 20),
            cost_estimate=pl.CostEstimate(
                flops=2 * rows * half_width * both // halves,
                bytes_accessed=2 * rows * half_width // halves,
                transcendentals=0,
            ),
            name="shrink",
        )(block_count, near_hidden, *(arrived[at] for at in mine_at), *parts)
    shrunk, up = parts
    shrunk_other = lax.ppermute(shrunk, "tp", swap)

    return pl.pallas_call(
        functools.partial(expand_kernel, slot_count, rank),
        out_shape=jax.ShapeDtypeStruct((step_count, row_count, share), bf16),
        in_specs=[VMEM] * 5,
        out_specs=ANY,
        scratch_shapes=[
            pltpu.VMEM((step_count, row_count, share), bf16),
            pltpu.SemaphoreType.DMA((step_count,)),
        ],
        compiler_params=pltpu.CompilerParams(vmem_limit_bytes=12 << 20),
        name="expand",
    )(shrunk, shrunk_other, up, mine, base_other)


def solution(mesh):
    in_specs = (
        P(None, ("rep", "grp"), "tp"),
        P("tp", None),
        P("grp", "tp", None),
        P("grp", None, None),
        P(),
        P("rep", None),
        P("rep"),
    )
    out_specs = P(None, ("rep", "grp"), "tp")
    return jax.shard_map(local, mesh=mesh, in_specs=in_specs, out_specs=out_specs, check_vma=False)
```
